32 devices in a mesh: tm: 16 (over z, y, x), rows: 2 (over core).
Axes of the slice: x: 2, y: 2, z: 4, core: 2. Of those that a mesh axis runs over, the one named last changes fastest.
Arguments:
- site_rates: float32 [256], replicated, may hold values from 0.0005 to 0.2
- prior_mean: float32 [512, 384], replicated, may hold values from -6 to 6
- observed: float32 [16, 256, 384], P('tm'), may hold values from -6 to 6
- obs_mask: int32 [16, 256], P('tm'), may hold values 0 or 1
- filter_gains: float32 [16, 512, 256], P('tm', 'rows'), may hold values from -0.05 to 0.8, as said below
- smooth_gains: float32 [16, 512, 512], P('tm', 'rows'), may hold values from -0.02 to 1, as said below
Outputs:
- filtered: float32 [16, 512, 384], P('tm', 'rows')
- smoothed: float32 [16, 512, 384], P('tm', 'rows')
The draws below stay inside these ranges and needn't reach their ends.
Inputs may be any that keep to these rules, and one draw needn't show every extreme that they name: `filter_gains`: gain of each step; row 2i + c is component c of site i, column j a site. `smooth_gains`: smoother gain of each step; rows and columns are state entries.
All inputs are finite; a program needn't handle non-finite values. No bound on the sum of `obs_mask` on one device may be relied on, other than what follows from the above.
Results may differ from the reference program's by a relative error of at most 0.0003.
Values sent between devices are 32-bit elements; how exact they have to be, the bound alone decides.
No kernel may reach another device: no remote copies, remote signals or barrier semaphores. Data moves between devices by JAX's collectives and lax.ppermute only.
A program may use at most 128 MiB of HBM per device.

```python
import math
import jax
import jax.numpy as jnp
from jax import lax

SITES = 256
STATE = 512
PATHS = 384
TIME_STEPS = 16


def draw_filter_gains(key, part):
    noise_random_key, gain_key = jax.random.split(key)
    shape = (TIME_STEPS, STATE, SITES)
    noise = jnp.clip(jax.random.normal(noise_random_key, shape, jnp.float32), -4.0, 4.0)
    level = jnp.exp(jax.random.uniform(gain_key, shape, jnp.float32, math.log(0.2), math.log(0.8)))
    row_ids = jnp.arange(STATE)[:, None]
    col_ids = jnp.arange(SITES)[None, :]
    own_site = row_ids // 2 == col_ids
    diagonal_entries = jnp.where(row_ids % 2 == 0, level, 0.02 * level)
    return jnp.where(own_site[None], diagonal_entries, noise * (0.06 / math.sqrt(SITES))).astype(jnp.float32)


def draw_smooth_gains(key, part):
    rate_key = jax.random.fold_in(key, 7)
    location_key = jax.random.fold_in(key, 11)
    noise_random_key, perturbation_key, spike_random_key = jax.random.split(key, 3)
    shape = (TIME_STEPS, STATE, STATE)
    damping_rates = jnp.exp(jax.random.uniform(rate_key, (1, STATE), jnp.float32, math.log(0.0005), math.log(0.1)))
    noise = jnp.clip(jax.random.normal(noise_random_key, shape, jnp.float32), -4.0, 4.0)
    small_perturbation = jax.random.uniform(perturbation_key, (TIME_STEPS, STATE), jnp.float32, 0.5, 1.5)
    spike_time_steps = jax.random.randint(location_key, (3,), 0, TIME_STEPS)
    spike_extent = jax.random.uniform(spike_random_key, (3,), jnp.float32, 0.5, 0.8)
    spike_hits = jnp.arange(TIME_STEPS)[:, None] == spike_time_steps[None, :]
    spike_multiplier = jnp.prod(jnp.where(spike_hits, spike_extent[None, :], 1.0), axis=1, keepdims=True)
    diagonal_entries = jnp.exp(-damping_rates * small_perturbation) * spike_multiplier
    identity = jnp.arange(STATE)[:, None] == jnp.arange(STATE)[None, :]
    return jnp.where(identity[None], diagonal_entries[:, :, None], noise * (0.03 / math.sqrt(STATE))).astype(jnp.float32)


def touch_ends(result, rng, smallest, top_value):
    shape = result.shape
    place = [jax.random.randint(jax.random.fold_in(rng, axis), (), 0, shape[axis]) for axis in range(len(shape))]
    result = result.at[tuple(place)].set(smallest)
    longest = shape.index(max(shape))
    place[longest] = (place[longest] + 1) % shape[longest]
    return result.at[tuple(place)].set(top_value)


def level_of(key, dims, shards, least, high):
    def one(dim, blocks):
        steps = jax.random.uniform(jax.random.fold_in(jax.random.fold_in(key, 6), dim), (blocks,), jnp.float32, least / len(shards), high / len(shards))
        return jnp.repeat(jnp.exp(steps), dims[dim] // blocks).reshape((-1,) + (1,) * (len(dims) - dim - 1))

    gain = one(*shards[0])
    for cut in shards[1:]:
        gain = gain * one(*cut)
    return gain


def scatter_about(stream_key, dims, scale, limit, cuts=(), kind=jnp.bfloat16):
    drawn = scale * jax.random.normal(stream_key, dims, jnp.float32)
    if cuts:
        drawn = drawn * level_of(stream_key, dims, cuts, -0.22, 0.18)
    return jnp.clip(drawn, -limit, limit).astype(kind)


def setup_inputs(seed: int = 0) -> dict:
    arg_keys = jax.random.split(jax.random.key(seed), 7)
    site_rates = jnp.clip(jnp.exp(jax.random.uniform(arg_keys[0], (SITES,), jnp.float32, math.log(0.0005), math.log(0.2))), 0.0005, 0.2)
    prior_mean = scatter_about(arg_keys[1], (STATE, PATHS), 1.0, 6.0, (), jnp.float32)
    observed = scatter_about(arg_keys[2], (TIME_STEPS, SITES, PATHS), 1.0, 6.0, ((0, 16),), jnp.float32)
    obs_mask = touch_ends((jax.random.randint(arg_keys[3], (TIME_STEPS, SITES), 0, 2) < 1).astype(jnp.int32), jax.random.fold_in(arg_keys[3], 1), 0, 1)
    filter_gains = draw_filter_gains(jax.random.fold_in(arg_keys[6], 71), 0)
    smooth_gains = draw_smooth_gains(jax.random.fold_in(arg_keys[6], 71), 0)
    return {"site_rates": site_rates, "prior_mean": prior_mean, "observed": observed, "obs_mask": obs_mask, "filter_gains": filter_gains, "smooth_gains": smooth_gains}


def product(left, right):
    return jnp.dot(left, right, precision=lax.Precision.HIGHEST, preferred_element_type=jnp.float32)


def transition_blocks(site_rates):
    decay = jnp.exp(-site_rates)
    top = jnp.stack([decay * (1.0 + site_rates), decay], -1)
    bottom = jnp.stack([-decay * site_rates * site_rates, decay * (1.0 - site_rates)], -1)
    return jnp.stack([top, bottom], 1)


def apply_transition(values, site_rates):
    blocks = transition_blocks(site_rates)
    paired = values.reshape(site_rates.shape[0], 2, values.shape[-1])
    moved = jnp.einsum("scd,sdb->scb", blocks, paired, precision=lax.Precision.HIGHEST)
    return moved.reshape(values.shape)


def reference(site_rates, prior_mean, observed, obs_mask, filter_gains, smooth_gains):
    def forward(state_now, inputs):
        obs_step, mask_step, gain_step = inputs
        predicted = apply_transition(state_now, site_rates)
        values = predicted.reshape(SITES, 2, predicted.shape[-1])[:, 0, :]
        innovation = mask_step.astype(jnp.float32)[:, None] * (obs_step - values)
        updated = predicted + product(gain_step, innovation)
        return updated, updated

    _, filtered = lax.scan(forward, prior_mean, (observed, obs_mask, filter_gains))

    def backward(later, inputs):
        state_step, gain_step = inputs
        updated = state_step + product(gain_step, later - apply_transition(state_step, site_rates))
        return updated, updated

    _, earlier = lax.scan(backward, filtered[-1], (filtered[:-1], smooth_gains[:-1]), reverse=True)
    smoothed = jnp.concatenate([earlier, filtered[-1:]], 0)
    return (filtered, smoothed)
```

```python
import functools

import jax
import jax.numpy as jnp
from jax import lax
from jax.experimental import pallas as pl
from jax.experimental.pallas import tpu as pltpu
from jax.sharding import PartitionSpec as P

GROUP = 4
LANES = 128
BF16 = jnp.bfloat16
F32 = jnp.float32


def whole(count):
    return [pl.BlockSpec(memory_space=pltpu.VMEM)] * count


def call(kernel, operands, shapes, scratch=(), aliases=None, flops=0, bytes_accessed=0):
    return pl.pallas_call(
        kernel,
        out_shape=[jax.ShapeDtypeStruct(shape, dtype) for shape, dtype in shapes],
        in_specs=whole(len(operands)),
        out_specs=whole(len(shapes)),
        scratch_shapes=list(scratch),
        input_output_aliases=aliases or {},
        compiler_params=pltpu.CompilerParams(vmem_limit_bytes=24 << 20),
        cost_estimate=pl.CostEstimate(flops=flops, bytes_accessed=bytes_accessed, transcendentals=0),
    )(*operands)


def place():
    step = lax.axis_index("tm")
    return lax.div(step, GROUP), lax.rem(step, GROUP), lax.axis_index("rows")


def split(value):
    high = value.astype(BF16)
    return high, (value - high.astype(F32)).astype(BF16)


def multiply(value, high_ref, low_ref):
    high, low = split(value)
    count = value.shape[0]
    both = jnp.dot(jnp.concatenate([high, low], 0), high_ref, preferred_element_type=F32)
    return both[:count] + both[count:] + jnp.dot(high, low_ref, preferred_element_type=F32)


def transition(state, coef_ref, half):
    values, slopes = [], []
    for block in range(state.shape[1] // (2 * half)):
        at = 2 * half * block
        value, slope = state[:, at : at + half], state[:, at + half : at + 2 * half]
        lanes = slice(block * half, (block + 1) * half)
        values.append(coef_ref[0:1, lanes] * value + coef_ref[1:2, lanes] * slope)
        slopes.append(coef_ref[2:3, lanes] * value + coef_ref[3:4, lanes] * slope)
    moved = jnp.concatenate([part for pair in zip(values, slopes) for part in pair], 1)
    return moved, jnp.concatenate(values, 1)


def lane_tiles(value):
    return [value[:, at : at + LANES] for at in range(0, value.shape[1], LANES)]


def gain_kernel(
    share, rates_ref, mask_ref, gain_ref, obs_ref, first_ref, second_ref, own_ref, coef_ref, turned, tiles
):
    _, spot, row = place()
    panel, sites = gain_ref.shape
    half = panel // 2
    mask = mask_ref[...].astype(F32)
    for at, tile in enumerate(lane_tiles(gain_ref[...] * mask)):
        tiles[at] = tile
        lines = slice(at * LANES, (at + 1) * LANES)
        for part in range(2):
            piece = tiles[at, pl.ds(part, half, stride=2), :].T
            lanes = slice(part * half, (part + 1) * half)
            first_ref[lines, lanes] = piece
            second_ref[lines, lanes] = piece
    turned[...] = obs_ref[...].T
    rows = lax.axis_size("rows")

    def slice_for(flip):
        start = (jnp.bitwise_xor(spot, flip) * rows + row) * share
        return turned[pl.ds(pl.multiple_of(start, 8), share), :]

    first_ref[sites : sites + share, :] = slice_for(1 + row)
    first_ref[sites + share : sites + 2 * share, :] = slice_for(3)
    second_ref[sites : sites + share, :] = slice_for(2 - row)
    own_ref[...] = slice_for(0)
    rate = rates_ref[...]
    decay = jnp.exp(-rate)
    coef_ref[0:1, :] = decay * (1.0 + rate)
    coef_ref[1:2, :] = decay
    coef_ref[2:3, :] = -decay * rate * rate
    coef_ref[3:4, :] = decay * (1.0 - rate)
    coef_ref[4:8, :] = jnp.zeros((4, sites), F32)


def prior_kernel(share, half, prior_ref, out_ref, turned, tiles):
    _, spot, row = place()
    rows = lax.axis_size("rows")
    for at, tile in enumerate(lane_tiles(prior_ref[...])):
        tiles[at] = tile
        for block in range(prior_ref.shape[0] // half):
            start = (block // 2) * 2 * half + block % 2
            piece = tiles[at, pl.ds(start, half, stride=2), :].T
            turned[at * LANES : (at + 1) * LANES, block * half : (block + 1) * half] = piece
    start = (spot * rows + row) * share
    out_ref[...] = turned[pl.ds(pl.multiple_of(start, 8), share), :]


def smoother_gain_kernel(gain_ref, out_ref, turned, tiles):
    panel, states = gain_ref.shape
    half = panel // 2
    for at, tile in enumerate(lane_tiles(gain_ref[...])):
        tiles[at] = tile
        for part in range(2):
            turned[part, at * LANES : (at + 1) * LANES, :] = tiles[at, pl.ds(part, half, stride=2), :].T
    for block in range(states // half):
        start = (block // 2) * 2 * half + block % 2
        for part in range(2):
            piece = turned[part, pl.ds(start, half, stride=2), :]
            out_ref[block * half : (block + 1) * half, part * half : (part + 1) * half] = piece


def gather_kernel(share, depth, own, a, b, d, other, other_a, other_b, other_d, *rest):
    _, spot, row = place()
    high_ref, low_ref = rest[-2 - (share > 0)], rest[-1 - (share > 0)]
    for ref, flip, block in (
        (own, 0, row),
        (a, 1 + row, row),
        (b, 2 - row, row),
        (d, 3, row),
        (other, 0, 1 - row),
        (other_a, 2 - row, 1 - row),
        (other_b, 1 + row, 1 - row),
        (other_d, 3, 1 - row),
    ):
        at = jnp.bitwise_xor(spot, flip)
        high, low = split(ref[0:depth, :])
        high_ref[at, block] = high
        low_ref[at, block] = low
    if share:
        own_obs, obs_ref = rest[0], rest[-1]
        obs_ref[spot] = own_obs[...]
        obs_ref[jnp.bitwise_xor(spot, 1 + row)] = a[depth : depth + share, :]
        obs_ref[jnp.bitwise_xor(spot, 2 - row)] = b[depth : depth + share, :]
        obs_ref[jnp.bitwise_xor(spot, 3)] = d[depth + share : depth + 2 * share, :]


def filter_kernel(turn, start_ref, coef_ref, high_ref, low_ref, obs_ref, *rest):
    out_ref, last_ref = rest[-2:]
    group, _, _ = place()
    half = high_ref.shape[3] // 2

    @pl.when(group == turn)
    def _():
        state = start_ref[...]
        for step in range(GROUP):
            moved, values = transition(state, coef_ref, half)
            innovation = obs_ref[step] - values
            update = [
                multiply(innovation, high_ref[step, block], low_ref[step, block])
                for block in range(high_ref.shape[1])
            ]
            state = moved + jnp.concatenate(update, 1)
            out_ref[step] = state
        last_ref[...] = state


def smooth_kernel(turn, groups, start_ref, coef_ref, high_ref, low_ref, filt_ref, *rest):
    mine, other, first_ref = rest[-9:-5], rest[-5:-1], rest[-1]
    group, spot, row = place()
    blocks, lanes = high_ref.shape[1], high_ref.shape[3]
    half = lanes // 2

    def pack(step, kind, state):
        near = jnp.where(row == 0, state[:, :lanes], state[:, lanes:])
        far = jnp.where(row == 0, state[:, lanes:], state[:, :lanes])
        for flip in range(GROUP):

            @pl.when(spot == (step ^ flip))
            def _():
                mine[flip][kind] = near
                other[flip][kind] = far

    @pl.when(group == groups - 1 - turn)
    def _():
        state = start_ref[...]
        for step in range(GROUP - 1, -1, -1):
            filt = filt_ref[step]
            if turn == 0 and step == GROUP - 1:
                state = filt
            else:
                change = state - transition(filt, coef_ref, half)[0]
                update = [multiply(change, high_ref[step, block], low_ref[step, block]) for block in range(blocks)]
                state = filt + jnp.concatenate(update, 1)
            pack(step, 0, filt)
            pack(step, 1, state)
        first_ref[...] = state


def home_kernel(share, m0, m1, m2, m3, o0, o1, o2, o3, filt_ref, smooth_ref, turned, tiles):
    _, spot, row = place()
    rows = lax.axis_size("rows")
    half = filt_ref.shape[0] // 2
    for flip, (near, far) in enumerate(((m0, o0), (m1, o1), (m2, o2), (m3, o3))):
        start = jnp.bitwise_xor(spot, flip) * rows
        for kind in range(2):
            turned[kind, pl.ds(pl.multiple_of((start + row) * share, 8), share), :] = near[kind]
            turned[kind, pl.ds(pl.multiple_of((start + 1 - row) * share, 8), share), :] = far[kind]
    for kind, ref in enumerate((filt_ref, smooth_ref)):
        for at in range(ref.shape[1] // LANES):
            lines = slice(at * LANES, (at + 1) * LANES)
            for part in range(2):
                piece = turned[kind, lines, part * half : (part + 1) * half].T
                tiles[kind, at, pl.ds(part, half, stride=2), :] = piece
            ref[:, lines] = tiles[kind, at]


def after(value, other):
    return lax.optimization_barrier((value, other))[0]


def body(site_rates, prior_mean, observed, obs_mask, filter_gains, smooth_gains):
    count, rows = lax.axis_size("tm"), lax.axis_size("rows")
    groups = count // GROUP
    panel, sites = filter_gains.shape[1:]
    states, paths = prior_mean.shape
    half = panel // 2
    share = paths // (GROUP * rows)
    both = ("tm", "rows")

    def swap(value, target):
        pairs = [(t * rows + r, target(t, r)) for t in range(count) for r in range(rows)]
        return lax.ppermute(value, both, pairs)

    def across(value, flip, core=0):
        return swap(value, lambda t, r: (t ^ flip) * rows + (r ^ core))

    def first_way(value):
        return swap(value, lambda t, r: (t ^ (1 + r)) * rows + r)

    def second_way(value):
        return swap(value, lambda t, r: (t ^ (2 - r)) * rows + r)

    def hop(value, source, target):
        pairs = [
            ((source * GROUP + m) * rows + r, (target * GROUP + m) * rows + r) for m in range(GROUP) for r in range(rows)
        ]
        return lax.ppermute(value, both, pairs)

    def exchange(first, second):
        own_x = across(first, 0, 1)
        a, b = first_way(first), second_way(second)
        d = second_way(a)
        return (first, a, b, d, own_x, across(a, 0, 1), across(b, 0, 1), across(d, 0, 1))

    message, second, own_obs, coef = call(
        functools.partial(gain_kernel, share),
        (site_rates.reshape(1, sites), obs_mask, filter_gains[0], observed[0]),
        [((sites + 2 * share, panel), F32), ((sites + share, panel), F32), ((share, sites), F32), ((8, sites), F32)],
        [pltpu.VMEM((paths, sites), F32), pltpu.VMEM((sites // LANES, panel, LANES), F32)],
    )
    gains = exchange(message, second)
    (prior,) = call(
        functools.partial(prior_kernel, share, half),
        (prior_mean,),
        [((share, states), F32)],
        [pltpu.VMEM((paths, states), F32), pltpu.VMEM((paths // LANES, states, LANES), F32)],
    )
    (turned_gain,) = call(
        smoother_gain_kernel,
        (smooth_gains[0],),
        [((states, panel), F32)],
        [pltpu.VMEM((2, states, half), F32), pltpu.VMEM((states // LANES, panel, LANES), F32)],
    )
    turned_gain = after(turned_gain, gains[3])
    smooth_parts = exchange(turned_gain, turned_gain)

    high, low, obs = call(
        functools.partial(gather_kernel, share, sites),
        (*gains, own_obs),
        [((GROUP, rows, sites, panel), BF16)] * 2 + [((GROUP, share, sites), F32)],
    )
    start, filtered = prior, None
    for turn in range(groups):
        operands = (start, coef, high, low, obs) + (() if filtered is None else (filtered,))
        filtered, last = call(
            functools.partial(filter_kernel, turn),
            operands,
            [((GROUP, share, states), F32), ((share, states), F32)],
            aliases=None if filtered is None else {5: 0},
        )
        if turn < groups - 1:
            start = hop(last, turn, turn + 1)

    high, low = call(
        functools.partial(gather_kernel, 0, states),
        smooth_parts,
        [((GROUP, rows, states, panel), BF16)] * 2,
    )
    start, packed = last, ()
    for turn in range(groups):
        *packed, first = call(
            functools.partial(smooth_kernel, turn, groups),
            (start, coef, high, low, filtered, *packed),
            [((2, share, panel), F32)] * (2 * GROUP) + [((share, states), F32)],
            aliases={5 + i: i for i in range(len(packed))},
        )
        if turn < groups - 1:
            start = hop(first, groups - 1 - turn, groups - 2 - turn)
    mine = [packed[0]] + [across(packed[flip], flip) for flip in range(1, GROUP)]
    other = [across(packed[GROUP + flip], flip, 1) for flip in range(GROUP)]
    filt, smooth = call(
        functools.partial(home_kernel, share),
        (*mine, *other),
        [((panel, paths), F32)] * 2,
        [pltpu.VMEM((2, paths, panel), F32), pltpu.VMEM((2, paths // LANES, panel, LANES), F32)],
    )
    return filt[None], smooth[None]


def solution(mesh):
    placed = (
        P(),
        P(),
        P("tm", None, None),
        P("tm", None),
        P("tm", "rows", None),
        P("tm", "rows", None),
    )
    return jax.shard_map(
        body,
        mesh=mesh,
        in_specs=placed,
        out_specs=(P("tm", "rows", None), P("tm", "rows", None)),
        check_vma=False,
    )
```

```python
import functools

import jax
import jax.numpy as jnp
from jax import lax
from jax.experimental import pallas as pl
from jax.experimental.pallas import tpu as pltpu
from jax.sharding import PartitionSpec as P

GROUP = 4
LANES = 128
PIECES = 1
FW = (0, 0, 10**11, 10**11)
BW = (0, 0, 10**10, 10**10)
G1 = G2 = G3 = 10**9
G4 = 10**9
G5 = 10**10
BF16 = jnp.bfloat16
F32 = jnp.float32


def call(kernel, operands, shapes, scratch=(), aliases=None, source=pltpu.VMEM, bytes_accessed=2 << 20, flops=0, grant=24 << 20):
    return pl.pallas_call(
        kernel,
        out_shape=[jax.ShapeDtypeStruct(shape, dtype) for shape, dtype in shapes],
        in_specs=[pl.BlockSpec(memory_space=source)] * len(operands),
        out_specs=[pl.BlockSpec(memory_space=pltpu.VMEM)] * len(shapes),
        scratch_shapes=list(scratch),
        input_output_aliases=aliases or {},
        compiler_params=pltpu.CompilerParams(vmem_limit_bytes=grant),
        cost_estimate=pl.CostEstimate(flops=flops, bytes_accessed=bytes_accessed, transcendentals=0),
    )(*operands)


def place():
    step = lax.axis_index("tm")
    return lax.div(step, GROUP), lax.rem(step, GROUP), lax.axis_index("rows")


def split(value):
    high = value.astype(BF16)
    return high, (value - high.astype(F32)).astype(BF16)


def multiply(value, high_ref, low_ref):
    high, low = split(value)
    count = value.shape[0]
    both = jnp.dot(jnp.concatenate([high, low], 0), high_ref, preferred_element_type=F32)
    return both[:count] + both[count:] + jnp.dot(high, low_ref, preferred_element_type=F32)


def transition(state, coef_ref, half):
    values, slopes = [], []
    for block in range(state.shape[1] // (2 * half)):
        at = 2 * half * block
        value, slope = state[:, at : at + half], state[:, at + half : at + 2 * half]
        lanes = slice(block * half, (block + 1) * half)
        values.append(coef_ref[0:1, lanes] * value + coef_ref[1:2, lanes] * slope)
        slopes.append(coef_ref[2:3, lanes] * value + coef_ref[3:4, lanes] * slope)
    moved = jnp.concatenate([part for pair in zip(values, slopes) for part in pair], 1)
    return moved, jnp.concatenate(values, 1)


def lane_tiles(value):
    return [value[:, at : at + LANES] for at in range(0, value.shape[1], LANES)]


def fetch(source, target, sem):
    copy = pltpu.make_async_copy(source, target, sem)
    copy.start()
    return copy


def gain_kernel(
    share,
    rates_hbm,
    mask_hbm,
    gain_hbm,
    obs_hbm,
    first_ref,
    second_ref,
    third_ref,
    own_ref,
    coef_ref,
    rates_ref,
    mask_ref,
    gain_ref,
    obs_ref,
    turned,
    tiles,
    sems,
):
    sent = (first_ref, second_ref, third_ref)
    copies = [
        fetch(source, target, sems.at[at])
        for at, (source, target) in enumerate(
            ((mask_hbm, mask_ref), (gain_hbm, gain_ref), (obs_hbm, obs_ref), (rates_hbm, rates_ref))
        )
    ]
    _, spot, row = place()
    panel, sites = gain_ref.shape
    half = panel // 2
    copies[0].wait()
    copies[1].wait()
    mask = mask_ref[...].astype(F32)
    for at, tile in enumerate(lane_tiles(gain_ref[...] * mask)):
        tiles[at] = tile
        lines = slice(at * LANES, (at + 1) * LANES)
        for part in range(2):
            piece = tiles[at, pl.ds(part, half, stride=2), :].T
            lanes = slice(part * half, (part + 1) * half)
            for ref in sent:
                ref[lines, lanes] = piece
    copies[2].wait()
    turned[...] = obs_ref[...].T
    rows = lax.axis_size("rows")

    def slice_for(flip):
        start = (jnp.bitwise_xor(spot, flip) * rows + row) * share
        return turned[pl.ds(pl.multiple_of(start, 8), share), :]

    for flip, ref in enumerate(sent, 1):
        ref[sites : sites + share, :] = slice_for(flip)
    own_ref[...] = slice_for(0)
    copies[3].wait()
    rate = rates_ref[...]
    decay = jnp.exp(-rate)
    coef_ref[0:1, :] = decay * (1.0 + rate)
    coef_ref[1:2, :] = decay
    coef_ref[2:3, :] = -decay * rate * rate
    coef_ref[3:4, :] = decay * (1.0 - rate)
    coef_ref[4:8, :] = jnp.zeros((4, sites), F32)


def prior_kernel(share, half, prior_ref, out_ref, turned, tiles):
    _, spot, row = place()
    rows = lax.axis_size("rows")
    for at, tile in enumerate(lane_tiles(prior_ref[...])):
        tiles[at] = tile
        for block in range(prior_ref.shape[0] // half):
            start = (block // 2) * 2 * half + block % 2
            piece = tiles[at, pl.ds(start, half, stride=2), :].T
            turned[at * LANES : (at + 1) * LANES, block * half : (block + 1) * half] = piece
    start = (spot * rows + row) * share
    out_ref[...] = turned[pl.ds(pl.multiple_of(start, 8), share), :]


def smoother_gain_kernel(gain_ref, *refs):
    parts, (turned, tiles) = refs[:-2], refs[-2:]
    depth = parts[0].shape[0]
    panel, states = gain_ref.shape
    half = panel // 2
    for at, tile in enumerate(lane_tiles(gain_ref[...])):
        tiles[at] = tile
        for part in range(2):
            turned[part, at * LANES : (at + 1) * LANES, :] = tiles[at, pl.ds(part, half, stride=2), :].T
    for block in range(states // half):
        start = (block // 2) * 2 * half + block % 2
        for part in range(2):
            piece = turned[part, pl.ds(start, half, stride=2), :]
            at = block * half % depth
            parts[block * half // depth][at : at + half, part * half : (part + 1) * half] = piece


def gather_kernel(share, depth, *refs):
    _, spot, row = place()
    near, far, rest = refs[:GROUP], refs[GROUP : 2 * GROUP], refs[2 * GROUP :]
    high_ref, low_ref = rest[-2 - (share > 0)], rest[-1 - (share > 0)]
    for flip in range(GROUP):
        at = jnp.bitwise_xor(spot, flip)
        for ref, block in ((near[flip], row), (far[flip], 1 - row)):
            high, low = split(ref[0:depth, :])
            high_ref[at, block] = high
            low_ref[at, block] = low
    if share:
        rest[-1][spot] = rest[0][...]
        for flip in range(1, GROUP):
            rest[-1][jnp.bitwise_xor(spot, flip)] = near[flip][depth : depth + share, :]


def choose_kernel(first_ref, second_ref, out_ref):
    _, _, row = place()

    @pl.when(row == 0)
    def _():
        out_ref[...] = first_ref[...]

    @pl.when(row != 0)
    def _():
        out_ref[...] = second_ref[...]


def pack(spot, step, refs, state):
    for flip, ref in enumerate(refs):

        @pl.when(spot == (step ^ flip))
        def _():
            ref[...] = state


def filter_kernel(turn, start_ref, coef_ref, high_ref, low_ref, obs_ref, *rest):
    out_ref, sent, last_ref = rest[-GROUP - 2], rest[-GROUP - 1 : -1], rest[-1]
    group, spot, _ = place()
    half = high_ref.shape[3] // 2

    @pl.when(group == turn)
    def _():
        state = start_ref[...]
        for step in range(GROUP):
            moved, values = transition(state, coef_ref, half)
            innovation = obs_ref[step] - values
            update = [
                multiply(innovation, high_ref[step, block], low_ref[step, block])
                for block in range(high_ref.shape[1])
            ]
            state = moved + jnp.concatenate(update, 1)
            out_ref[step] = state
            pack(spot, step, sent, state)
        last_ref[...] = state


def smooth_kernel(turn, groups, start_ref, coef_ref, high_ref, low_ref, filt_ref, *rest):
    sent, first_ref = rest[-GROUP - 1 : -1], rest[-1]
    group, spot, _ = place()
    half = high_ref.shape[3] // 2

    @pl.when(group == groups - 1 - turn)
    def _():
        state = start_ref[...]
        for step in range(GROUP - 1, -1, -1):
            filt = filt_ref[step]
            if turn == 0 and step == GROUP - 1:
                state = filt
            else:
                change = state - transition(filt, coef_ref, half)[0]
                update = [
                    multiply(change, high_ref[step, block], low_ref[step, block])
                    for block in range(high_ref.shape[1])
                ]
                state = filt + jnp.concatenate(update, 1)
            pack(spot, step, sent, state)
        first_ref[...] = state


def home_kernel(share, *refs):
    near, far, (out_ref, turned, tiles) = refs[:GROUP], refs[GROUP : 2 * GROUP], refs[2 * GROUP :]
    _, spot, row = place()
    rows = lax.axis_size("rows")
    half = out_ref.shape[0] // 2
    lanes = pl.ds(pl.multiple_of(row * 2 * half, LANES), 2 * half)
    for flip in range(GROUP):
        start = jnp.bitwise_xor(spot, flip) * rows
        turned[pl.ds(pl.multiple_of((start + row) * share, 8), share), :] = near[flip][:, lanes]
        turned[pl.ds(pl.multiple_of((start + 1 - row) * share, 8), share), :] = far[flip][:, lanes]
    for at in range(out_ref.shape[1] // LANES):
        lines = slice(at * LANES, (at + 1) * LANES)
        for part in range(2):
            tiles[at, pl.ds(part, half, stride=2), :] = turned[lines, part * half : (part + 1) * half].T
        out_ref[:, lines] = tiles[at]


def gate(values, token, flops):
    return call(
        lambda *refs: None,
        (*values, token),
        [(value.shape, value.dtype) for value in values],
        aliases={at: at for at in range(len(values))},
        flops=flops,
    )


def body(site_rates, prior_mean, observed, obs_mask, filter_gains, smooth_gains):
    count, rows = lax.axis_size("tm"), lax.axis_size("rows")
    groups = count // GROUP
    panel, sites = filter_gains.shape[1:]
    states, paths = prior_mean.shape
    half = panel // 2
    share = paths // (GROUP * rows)
    both = ("tm", "rows")

    def swap(value, target):
        pairs = [(t * rows + r, target(t, r)) for t in range(count) for r in range(rows)]
        return lax.ppermute(value, both, pairs)

    def across(value, flip, core=0):
        return swap(value, lambda t, r: (t ^ flip) * rows + (r ^ core))

    def forward(value):
        return swap(value, lambda t, r: (t ^ (2 - r)) * rows + r)

    def neighbour(value):
        return across(value, 0, 1)

    def hop(value, source, target):
        pairs = [
            ((source * GROUP + m) * rows + r, (target * GROUP + m) * rows + r)
            for m in range(GROUP)
            for r in range(rows)
        ]
        return lax.ppermute(value, both, pairs)

    def send_home(sent):
        return [sent[0]] + [across(sent[flip], flip) for flip in range(1, GROUP)]

    def settle(near):
        (out,) = call(
            functools.partial(home_kernel, share),
            (*near, *[neighbour(value) for value in near]),
            [((panel, paths), F32)],
            [pltpu.VMEM((paths, panel), F32), pltpu.VMEM((paths // LANES, panel, LANES), F32)],
        )
        return out[None]

    *messages, own_obs, coef = call(
        functools.partial(gain_kernel, share),
        tuple(pltpu.with_memory_space_constraint(x, pltpu.HBM) for x in (site_rates.reshape(1, sites), obs_mask, filter_gains[0], observed[0])),
        [((sites + share, panel), F32)] * (GROUP - 1) + [((share, sites), F32), ((8, sites), F32)],
        [
            pltpu.VMEM((1, sites), F32),
            pltpu.VMEM((1, sites), jnp.int32),
            pltpu.VMEM((panel, sites), F32),
            pltpu.VMEM((sites, paths), F32),
            pltpu.VMEM((paths, sites), F32),
            pltpu.VMEM((sites // LANES, panel, LANES), F32),
            pltpu.SemaphoreType.DMA((4,)),
        ],
        source=pltpu.HBM,
    )
    near = [across(value, flip) for flip, value in enumerate(messages, 1)]
    (prior,) = call(
        functools.partial(prior_kernel, share, half),
        (prior_mean,),
        [((share, states), F32)],
        [pltpu.VMEM((paths, states), F32), pltpu.VMEM((paths // LANES, states, LANES), F32)],
    )
    pieces = call(
        smoother_gain_kernel,
        (smooth_gains[0],),
        [((states // PIECES, panel), F32)] * PIECES,
        [pltpu.VMEM((2, states, half), F32), pltpu.VMEM((states // LANES, panel, LANES), F32)],
    )
    (turned_gain,) = pieces
    gain_x, gain_y = across(turned_gain, 1), across(turned_gain, 2)
    own_far, prior = lax.optimization_barrier((neighbour(messages[0]), prior))
    *near, own_far, prior, turned_gain = lax.optimization_barrier((*near, own_far, prior, turned_gain))
    far = [own_far] + [neighbour(value) for value in near]
    near = [messages[0], *near]
    high, low, obs = call(
        functools.partial(gather_kernel, share, sites),
        (*near, *far, own_obs),
        [((GROUP, rows, sites, panel), BF16)] * 2 + [((GROUP, share, sites), F32)],
    )
    start, filtered = prior, ()
    for turn in range(groups):
        *filtered, last = call(
            functools.partial(filter_kernel, turn),
            (start, coef, high, low, obs, *filtered),
            [((GROUP, share, states), F32)] + [((share, states), F32)] * (GROUP + 1),
            aliases={5 + i: i for i in range(len(filtered))},
            flops=FW[min(turn,3)],
        )
        if turn < groups - 1:
            start = hop(last, turn, turn + 1)
        if turn == groups - 3:
            turned_gain, gain_x, gain_y = gate((turned_gain, gain_x, gain_y), last, G1)
            (gain_d,) = call(choose_kernel, (gain_x, gain_y), [((states, panel), F32)], flops=G1)
            gain_d = forward(gain_d)
            gain_near = list(gate((turned_gain, gain_x, gain_y), start, G2))
            gain_far = [neighbour(value) for value in gain_near]
        if turn == groups - 2:
            (gain_d,) = gate((gain_d,), gain_far[2], G3)
            gain_near.append(gain_d)
            gain_far.append(neighbour(gain_d))
    filtered, sent = filtered[0], filtered[1:]

    high, low = call(
        functools.partial(gather_kernel, 0, states),
        (*gain_near, *gain_far),
        [((GROUP, rows, states, panel), BF16)] * 2,
    )
    start, packed = last, ()
    for turn in range(groups):
        *packed, first = call(
            functools.partial(smooth_kernel, turn, groups),
            (start, coef, high, low, filtered, *packed),
            [((share, states), F32)] * (GROUP + 1),
            aliases={5 + i: i for i in range(len(packed))},
            flops=BW[min(turn,3)],
        )
        if turn < groups - 1:
            start = hop(first, groups - 1 - turn, groups - 2 - turn)
        if turn == groups - 2:
            filt_near = send_home(gate(sent, first, G4))
    smooth_near = send_home(packed)
    filt = settle(gate(filt_near, smooth_near[1], G5))
    smooth = settle(smooth_near)
    return filt, smooth


def solution(mesh):
    placed = (
        P(),
        P(),
        P("tm", None, None),
        P("tm", None),
        P("tm", "rows", None),
        P("tm", "rows", None),
    )
    return jax.shard_map(
        body,
        mesh=mesh,
        in_specs=placed,
        out_specs=(P("tm", "rows", None), P("tm", "rows", None)),
        check_vma=False,
    )
```

```python
import functools

import jax
import jax.numpy as jnp
from jax import lax
from jax.experimental import pallas as pl
from jax.experimental.pallas import tpu as pltpu
from jax.sharding import PartitionSpec as P

GROUP = 4
LANES = 128
PIECES = 1
FW = (0, 0, 10**11, 10**11)
BW = (0, 10**10)
JF = 10**11
G1 = G2 = G3 = 10**9
G4 = 10**9
G6 = 10**9
G5 = 10**10
BF16 = jnp.bfloat16
F32 = jnp.float32


def call(kernel, operands, shapes, scratch=(), aliases=None, source=pltpu.VMEM, bytes_accessed=2 << 20, flops=0, grant=24 << 20):
    return pl.pallas_call(
        kernel,
        out_shape=[jax.ShapeDtypeStruct(shape, dtype) for shape, dtype in shapes],
        in_specs=[pl.BlockSpec(memory_space=source)] * len(operands),
        out_specs=[pl.BlockSpec(memory_space=pltpu.VMEM)] * len(shapes),
        scratch_shapes=list(scratch),
        input_output_aliases=aliases or {},
        compiler_params=pltpu.CompilerParams(vmem_limit_bytes=grant),
        cost_estimate=pl.CostEstimate(flops=flops, bytes_accessed=bytes_accessed, transcendentals=0),
    )(*operands)


def place():
    step = lax.axis_index("tm")
    return lax.div(step, GROUP), lax.rem(step, GROUP), lax.axis_index("rows")


def split(value):
    high = value.astype(BF16)
    return high, (value - high.astype(F32)).astype(BF16)


def multiply(value, high_ref, low_ref):
    high, low = split(value)
    count = value.shape[0]
    both = jnp.dot(jnp.concatenate([high, low], 0), high_ref, preferred_element_type=F32)
    return both[:count] + both[count:] + jnp.dot(high, low_ref, preferred_element_type=F32)


def transition(state, coef_ref, half):
    values, slopes = [], []
    for block in range(state.shape[1] // (2 * half)):
        at = 2 * half * block
        value, slope = state[:, at : at + half], state[:, at + half : at + 2 * half]
        lanes = slice(block * half, (block + 1) * half)
        values.append(coef_ref[0:1, lanes] * value + coef_ref[1:2, lanes] * slope)
        slopes.append(coef_ref[2:3, lanes] * value + coef_ref[3:4, lanes] * slope)
    moved = jnp.concatenate([part for pair in zip(values, slopes) for part in pair], 1)
    return moved, jnp.concatenate(values, 1)


def lane_tiles(value):
    return [value[:, at : at + LANES] for at in range(0, value.shape[1], LANES)]


def fetch(source, target, sem):
    copy = pltpu.make_async_copy(source, target, sem)
    copy.start()
    return copy


def gain_kernel(
    share,
    rates_hbm,
    mask_hbm,
    gain_hbm,
    obs_hbm,
    first_ref,
    second_ref,
    third_ref,
    own_ref,
    coef_ref,
    rates_ref,
    mask_ref,
    gain_ref,
    obs_ref,
    turned,
    tiles,
    sems,
):
    sent = (first_ref, second_ref, third_ref)
    copies = [
        fetch(source, target, sems.at[at])
        for at, (source, target) in enumerate(
            ((mask_hbm, mask_ref), (gain_hbm, gain_ref), (obs_hbm, obs_ref), (rates_hbm, rates_ref))
        )
    ]
    _, spot, row = place()
    panel, sites = gain_ref.shape
    half = panel // 2
    copies[0].wait()
    copies[1].wait()
    mask = mask_ref[...].astype(F32)
    for at, tile in enumerate(lane_tiles(gain_ref[...] * mask)):
        tiles[at] = tile
        lines = slice(at * LANES, (at + 1) * LANES)
        for part in range(2):
            piece = tiles[at, pl.ds(part, half, stride=2), :].T
            lanes = slice(part * half, (part + 1) * half)
            for ref in sent:
                ref[lines, lanes] = piece
    copies[2].wait()
    turned[...] = obs_ref[...].T
    rows = lax.axis_size("rows")

    def slice_for(flip):
        start = (jnp.bitwise_xor(spot, flip) * rows + row) * share
        return turned[pl.ds(pl.multiple_of(start, 8), share), :]

    for flip, ref in enumerate(sent, 1):
        ref[sites : sites + share, :] = slice_for(flip)
    own_ref[...] = slice_for(0)
    copies[3].wait()
    rate = rates_ref[...]
    decay = jnp.exp(-rate)
    coef_ref[0:1, :] = decay * (1.0 + rate)
    coef_ref[1:2, :] = decay
    coef_ref[2:3, :] = -decay * rate * rate
    coef_ref[3:4, :] = decay * (1.0 - rate)
    coef_ref[4:8, :] = jnp.zeros((4, sites), F32)


def prior_kernel(share, half, prior_ref, out_ref, turned, tiles):
    _, spot, row = place()
    rows = lax.axis_size("rows")
    for at, tile in enumerate(lane_tiles(prior_ref[...])):
        tiles[at] = tile
        for block in range(prior_ref.shape[0] // half):
            start = (block // 2) * 2 * half + block % 2
            piece = tiles[at, pl.ds(start, half, stride=2), :].T
            turned[at * LANES : (at + 1) * LANES, block * half : (block + 1) * half] = piece
    start = (spot * rows + row) * share
    out_ref[...] = turned[pl.ds(pl.multiple_of(start, 8), share), :]


def smoother_gain_kernel(gain_ref, *refs):
    parts, (turned, tiles) = refs[:-2], refs[-2:]
    depth = parts[0].shape[0]
    panel, states = gain_ref.shape
    half = panel // 2
    for at, tile in enumerate(lane_tiles(gain_ref[...])):
        tiles[at] = tile
        for part in range(2):
            turned[part, at * LANES : (at + 1) * LANES, :] = tiles[at, pl.ds(part, half, stride=2), :].T
    for block in range(states // half):
        start = (block // 2) * 2 * half + block % 2
        for part in range(2):
            piece = turned[part, pl.ds(start, half, stride=2), :]
            at = block * half % depth
            parts[block * half // depth][at : at + half, part * half : (part + 1) * half] = piece


def gather_kernel(share, depth, *refs):
    _, spot, row = place()
    near, far, rest = refs[:GROUP], refs[GROUP : 2 * GROUP], refs[2 * GROUP :]
    high_ref, low_ref = rest[-2 - (share > 0)], rest[-1 - (share > 0)]
    for flip in range(GROUP):
        at = jnp.bitwise_xor(spot, flip)
        for ref, block in ((near[flip], row), (far[flip], 1 - row)):
            high, low = split(ref[0:depth, :])
            high_ref[at, block] = high
            low_ref[at, block] = low
    if share:
        rest[-1][spot] = rest[0][...]
        for flip in range(1, GROUP):
            rest[-1][jnp.bitwise_xor(spot, flip)] = near[flip][depth : depth + share, :]


def choose_kernel(first_ref, second_ref, out_ref):
    _, _, row = place()

    @pl.when(row == 0)
    def _():
        out_ref[...] = first_ref[...]

    @pl.when(row != 0)
    def _():
        out_ref[...] = second_ref[...]


def pack(spot, step, refs, state):
    for flip, ref in enumerate(refs):

        @pl.when(spot == (step ^ flip))
        def _():
            ref[...] = state


def filter_kernel(turn, start_ref, coef_ref, high_ref, low_ref, obs_ref, *rest):
    out_ref, sent, last_ref = rest[-GROUP - 2], rest[-GROUP - 1 : -1], rest[-1]
    group, spot, _ = place()
    half = high_ref.shape[3] // 2

    @pl.when(group == turn)
    def _():
        state = start_ref[...]
        for step in range(GROUP):
            moved, values = transition(state, coef_ref, half)
            innovation = obs_ref[step] - values
            update = [
                multiply(innovation, high_ref[step, block], low_ref[step, block])
                for block in range(high_ref.shape[1])
            ]
            state = moved + jnp.concatenate(update, 1)
            out_ref[step] = state
            pack(spot, step, sent, state)
        last_ref[...] = state


def smooth_steps(state, coef_ref, high_ref, low_ref, filt_ref, keep, last_group=False):
    half = high_ref.shape[3] // 2
    for step in range(GROUP - 1, -1, -1):
        filt = filt_ref[step]
        if last_group and step == GROUP - 1:
            state = filt
        else:
            change = state - transition(filt, coef_ref, half)[0]
            update = [
                multiply(change, high_ref[step, block], low_ref[step, block]) for block in range(high_ref.shape[1])
            ]
            state = filt + jnp.concatenate(update, 1)
        keep(step, state)
    return state


def smooth_kernel(turn, groups, start_ref, coef_ref, high_ref, low_ref, filt_ref, *rest):
    sent, first = (rest[-GROUP - 1 : -1], rest[-1:]) if turn == 0 else (rest[-GROUP:], ())
    group, spot, _ = place()

    @pl.when(group == groups - 1 - turn)
    def _():
        keep = lambda step, state: pack(spot, step, sent, state)
        state = smooth_steps(start_ref[...], coef_ref, high_ref, low_ref, filt_ref, keep, turn == 0)
        for ref in first:
            ref[...] = state


def joined_kernel(groups, coef_ref, high_ref, low_ref, filt_ref, map_high_ref, map_low_ref, offset_ref):
    group, _, _ = place()

    @pl.when(jnp.logical_and(group > 0, group < groups - 1))
    def _():
        blocks, lanes = high_ref.shape[1], high_ref.shape[3]
        nothing = jnp.zeros(offset_ref.shape, F32)
        offset_ref[...] = smooth_steps(nothing, coef_ref, high_ref, low_ref, filt_ref, lambda *_: None)
        last = GROUP - 1
        joined = [high_ref[last, block].astype(F32) + low_ref[last, block].astype(F32) for block in range(blocks)]
        for step in range(GROUP - 2, -1, -1):
            whole = jnp.concatenate(joined, 1)
            joined = [multiply(whole, high_ref[step, block], low_ref[step, block]) for block in range(blocks)]
        for block in range(blocks):
            map_high_ref[block], map_low_ref[block] = split(joined[block])


def jump_kernel(turn, groups, start_ref, map_high_ref, map_low_ref, offset_ref, first_ref):
    group, _, _ = place()

    @pl.when(group == groups - 1 - turn)
    def _():
        start = start_ref[...]
        moved = [multiply(start, map_high_ref[block], map_low_ref[block]) for block in range(map_high_ref.shape[0])]
        first_ref[...] = offset_ref[...] + jnp.concatenate(moved, 1)


def across_kernel(*refs):
    _, _, row = place()
    lanes = refs[-1].shape[2]
    for at, ref in enumerate(refs[:-1]):
        refs[-1][at] = ref[:, pl.ds(pl.multiple_of((1 - row) * lanes, LANES), lanes)]


def home_kernel(share, *refs):
    near, (far_ref, *outs, turned, tiles) = refs[: 2 * GROUP], refs[2 * GROUP :]
    _, spot, row = place()
    rows = lax.axis_size("rows")
    panel, paths = outs[0].shape
    half = panel // 2
    lanes = pl.ds(pl.multiple_of(row * panel, LANES), panel)
    for kind, out_ref in enumerate(outs):
        for flip in range(GROUP):
            at = kind * GROUP + flip
            start = jnp.bitwise_xor(spot, flip) * rows
            turned[kind, pl.ds(pl.multiple_of((start + row) * share, 8), share), :] = near[at][:, lanes]
            turned[kind, pl.ds(pl.multiple_of((start + 1 - row) * share, 8), share), :] = far_ref[at]
        for at in range(paths // LANES):
            lines = slice(at * LANES, (at + 1) * LANES)
            for part in range(2):
                piece = turned[kind, lines, part * half : (part + 1) * half].T
                tiles[kind, at, pl.ds(part, half, stride=2), :] = piece
            out_ref[:, lines] = tiles[kind, at]


def gate(values, token, flops):
    return call(
        lambda *refs: None,
        (*values, token),
        [(value.shape, value.dtype) for value in values],
        aliases={at: at for at in range(len(values))},
        flops=flops,
    )


def body(site_rates, prior_mean, observed, obs_mask, filter_gains, smooth_gains):
    count, rows = lax.axis_size("tm"), lax.axis_size("rows")
    groups = count // GROUP
    panel, sites = filter_gains.shape[1:]
    states, paths = prior_mean.shape
    half = panel // 2
    share = paths // (GROUP * rows)
    both = ("tm", "rows")

    def swap(value, target):
        pairs = [(t * rows + r, target(t, r)) for t in range(count) for r in range(rows)]
        return lax.ppermute(value, both, pairs)

    def across(value, flip):
        return swap(value, lambda t, r: (t ^ flip) * rows + r)

    def forward(value):
        return swap(value, lambda t, r: (t ^ (2 - r)) * rows + r)

    def neighbour(value):
        return swap(value, lambda t, r: t * rows + 1 - r)

    def hop(value, source, target):
        pairs = [
            ((source * GROUP + m) * rows + r, (target * GROUP + m) * rows + r)
            for m in range(GROUP)
            for r in range(rows)
        ]
        return lax.ppermute(value, both, pairs)

    def send_home(sent):
        return [across(sent[flip], flip) for flip in reversed(range(1, GROUP))][::-1]

    *messages, own_obs, coef = call(
        functools.partial(gain_kernel, share),
        tuple(pltpu.with_memory_space_constraint(x, pltpu.HBM) for x in (site_rates.reshape(1, sites), obs_mask, filter_gains[0], observed[0])),
        [((sites + share, panel), F32)] * (GROUP - 1) + [((share, sites), F32), ((8, sites), F32)],
        [
            pltpu.VMEM((1, sites), F32),
            pltpu.VMEM((1, sites), jnp.int32),
            pltpu.VMEM((panel, sites), F32),
            pltpu.VMEM((sites, paths), F32),
            pltpu.VMEM((paths, sites), F32),
            pltpu.VMEM((sites // LANES, panel, LANES), F32),
            pltpu.SemaphoreType.DMA((4,)),
        ],
        source=pltpu.HBM,
    )
    near = [across(value, flip) for flip, value in enumerate(messages, 1)]
    (prior,) = call(
        functools.partial(prior_kernel, share, half),
        (prior_mean,),
        [((share, states), F32)],
        [pltpu.VMEM((paths, states), F32), pltpu.VMEM((paths // LANES, states, LANES), F32)],
    )
    pieces = call(
        smoother_gain_kernel,
        (smooth_gains[0],),
        [((states // PIECES, panel), F32)] * PIECES,
        [pltpu.VMEM((2, states, half), F32), pltpu.VMEM((states // LANES, panel, LANES), F32)],
    )
    (turned_gain,) = pieces
    gain_x, gain_y = across(turned_gain, 1), across(turned_gain, 2)
    own_far, prior = lax.optimization_barrier((neighbour(messages[0]), prior))
    *near, own_far, prior, turned_gain = lax.optimization_barrier((*near, own_far, prior, turned_gain))
    far = [own_far] + [neighbour(value) for value in near]
    near = [messages[0], *near]
    high, low, obs = call(
        functools.partial(gather_kernel, share, sites),
        (*near, *far, own_obs),
        [((GROUP, rows, sites, panel), BF16)] * 2 + [((GROUP, share, sites), F32)],
    )
    start, filtered = prior, ()
    for turn in range(groups):
        *filtered, last = call(
            functools.partial(filter_kernel, turn),
            (start, coef, high, low, obs, *filtered),
            [((GROUP, share, states), F32)] + [((share, states), F32)] * (GROUP + 1),
            aliases={5 + i: i for i in range(len(filtered))},
            flops=FW[min(turn,3)],
        )
        if turn < groups - 1:
            start = hop(last, turn, turn + 1)
        if turn == groups - 3:
            turned_gain, gain_x, gain_y = gate((turned_gain, gain_x, gain_y), last, G1)
            (gain_d,) = call(choose_kernel, (gain_x, gain_y), [((states, panel), F32)], flops=G1)
            gain_d = forward(gain_d)
            gain_near = list(gate((turned_gain, gain_x, gain_y), start, G2))
            gain_far = [neighbour(value) for value in gain_near]
        if turn == groups - 2:
            (gain_d,) = gate((gain_d,), gain_far[2], G3)
            gain_near.append(gain_d)
            gain_far.append(neighbour(gain_d))
    filtered, sent = filtered[0], filtered[1:]

    high, low = call(
        functools.partial(gather_kernel, 0, states),
        (*gain_near, *gain_far),
        [((GROUP, rows, states, panel), BF16)] * 2,
    )
    start, packed = last, ()
    *joined, offset = call(
        functools.partial(joined_kernel, groups),
        (coef, high, low, filtered),
        [((rows, states, panel), BF16)] * 2 + [((share, states), F32)],
        flops=JF,
    )
    for turn in range(groups):
        middle = 0 < turn < groups - 1
        if middle:
            (first,) = call(
                functools.partial(jump_kernel, turn, groups), (start, *joined, offset), [((share, states), F32)]
            )
            here = hop(first, groups - 1 - turn, groups - 2 - turn)
        packed = call(
            functools.partial(smooth_kernel, turn, groups),
            (start, coef, high, low, filtered, *packed),
            [((share, states), F32)] * (GROUP + (turn == 0)),
            aliases={5 + i: i for i in range(len(packed))},
            flops=BW[1] if middle else BW[0],
        )
        if turn == 0:
            *packed, first = packed
            here = hop(first, groups - 1, groups - 2)
        if turn == groups - 2:
            sent = gate(sent, first, G4)
            sent = [sent[0], *send_home(sent)]
        if turn < groups - 1:
            start = here
    near = (*sent, packed[0], *send_home(packed))
    (far,) = call(across_kernel, near, [((2 * GROUP, share, panel), F32)])
    filt, smooth = call(
        functools.partial(home_kernel, share),
        (*near, neighbour(far)),
        [((panel, paths), F32)] * 2,
        [pltpu.VMEM((2, paths, panel), F32), pltpu.VMEM((2, paths // LANES, panel, LANES), F32)],
    )
    return filt[None], smooth[None]


def solution(mesh):
    placed = (
        P(),
        P(),
        P("tm", None, None),
        P("tm", None),
        P("tm", "rows", None),
        P("tm", "rows", None),
    )
    return jax.shard_map(
        body,
        mesh=mesh,
        in_specs=placed,
        out_specs=(P("tm", "rows", None), P("tm", "rows", None)),
        check_vma=False,
    )
```

```python
import functools

import jax
import jax.numpy as jnp
from jax import lax
from jax.experimental import pallas as pl
from jax.experimental.pallas import tpu as pltpu
from jax.sharding import PartitionSpec as P

GROUP = 4
LANES = 128
PIECES = 1
FW = (0, 0, 10**11, 10**11)
BW = (0, 10**10)
JF = 10**11
JP = 0
JJ = 0
GA = 10**10
AF = 0
G1 = G2 = G3 = 10**9
G4 = 10**9
G6 = 10**9
G5 = 10**10
BF16 = jnp.bfloat16
F32 = jnp.float32


def call(kernel, operands, shapes, scratch=(), aliases=None, source=pltpu.VMEM, bytes_accessed=2 << 20, flops=0, grant=24 << 20):
    return pl.pallas_call(
        kernel,
        out_shape=[jax.ShapeDtypeStruct(shape, dtype) for shape, dtype in shapes],
        in_specs=[pl.BlockSpec(memory_space=source)] * len(operands),
        out_specs=[pl.BlockSpec(memory_space=pltpu.VMEM)] * len(shapes),
        scratch_shapes=list(scratch),
        input_output_aliases=aliases or {},
        compiler_params=pltpu.CompilerParams(vmem_limit_bytes=grant),
        cost_estimate=pl.CostEstimate(flops=flops, bytes_accessed=bytes_accessed, transcendentals=0),
    )(*operands)


def place():
    step = lax.axis_index("tm")
    return lax.div(step, GROUP), lax.rem(step, GROUP), lax.axis_index("rows")


def split(value):
    high = value.astype(BF16)
    return high, (value - high.astype(F32)).astype(BF16)


def multiply(value, high_ref, low_ref):
    high, low = split(value)
    count = value.shape[0]
    both = jnp.dot(jnp.concatenate([high, low], 0), high_ref, preferred_element_type=F32)
    return both[:count] + both[count:] + jnp.dot(high, low_ref, preferred_element_type=F32)


def transition(state, coef_ref, half):
    values, slopes = [], []
    for block in range(state.shape[1] // (2 * half)):
        at = 2 * half * block
        value, slope = state[:, at : at + half], state[:, at + half : at + 2 * half]
        lanes = slice(block * half, (block + 1) * half)
        values.append(coef_ref[0:1, lanes] * value + coef_ref[1:2, lanes] * slope)
        slopes.append(coef_ref[2:3, lanes] * value + coef_ref[3:4, lanes] * slope)
    moved = jnp.concatenate([part for pair in zip(values, slopes) for part in pair], 1)
    return moved, jnp.concatenate(values, 1)


def lane_tiles(value):
    return [value[:, at : at + LANES] for at in range(0, value.shape[1], LANES)]


def fetch(source, target, sem):
    copy = pltpu.make_async_copy(source, target, sem)
    copy.start()
    return copy


def gain_kernel(
    share,
    rates_hbm,
    mask_hbm,
    gain_hbm,
    obs_hbm,
    first_ref,
    second_ref,
    third_ref,
    own_ref,
    coef_ref,
    rates_ref,
    mask_ref,
    gain_ref,
    obs_ref,
    turned,
    tiles,
    sems,
):
    sent = (first_ref, second_ref, third_ref)
    copies = [
        fetch(source, target, sems.at[at])
        for at, (source, target) in enumerate(
            ((mask_hbm, mask_ref), (gain_hbm, gain_ref), (obs_hbm, obs_ref), (rates_hbm, rates_ref))
        )
    ]
    _, spot, row = place()
    panel, sites = gain_ref.shape
    half = panel // 2
    copies[0].wait()
    copies[1].wait()
    mask = mask_ref[...].astype(F32)
    for at, tile in enumerate(lane_tiles(gain_ref[...] * mask)):
        tiles[at] = tile
        lines = slice(at * LANES, (at + 1) * LANES)
        for part in range(2):
            piece = tiles[at, pl.ds(part, half, stride=2), :].T
            lanes = slice(part * half, (part + 1) * half)
            for ref in sent:
                ref[lines, lanes] = piece
    copies[2].wait()
    turned[...] = obs_ref[...].T
    rows = lax.axis_size("rows")

    def slice_for(flip):
        start = (jnp.bitwise_xor(spot, flip) * rows + row) * share
        return turned[pl.ds(pl.multiple_of(start, 8), share), :]

    for flip, ref in enumerate(sent, 1):
        ref[sites : sites + share, :] = slice_for(flip)
    own_ref[...] = slice_for(0)
    copies[3].wait()
    rate = rates_ref[...]
    decay = jnp.exp(-rate)
    coef_ref[0:1, :] = decay * (1.0 + rate)
    coef_ref[1:2, :] = decay
    coef_ref[2:3, :] = -decay * rate * rate
    coef_ref[3:4, :] = decay * (1.0 - rate)
    coef_ref[4:8, :] = jnp.zeros((4, sites), F32)


def prior_kernel(share, half, prior_ref, out_ref, turned, tiles):
    _, spot, row = place()
    rows = lax.axis_size("rows")
    for at, tile in enumerate(lane_tiles(prior_ref[...])):
        tiles[at] = tile
        for block in range(prior_ref.shape[0] // half):
            start = (block // 2) * 2 * half + block % 2
            piece = tiles[at, pl.ds(start, half, stride=2), :].T
            turned[at * LANES : (at + 1) * LANES, block * half : (block + 1) * half] = piece
    start = (spot * rows + row) * share
    out_ref[...] = turned[pl.ds(pl.multiple_of(start, 8), share), :]


def smoother_gain_kernel(gain_ref, *refs):
    parts, (turned, tiles) = refs[:-2], refs[-2:]
    depth = parts[0].shape[0]
    panel, states = gain_ref.shape
    half = panel // 2
    for at, tile in enumerate(lane_tiles(gain_ref[...])):
        tiles[at] = tile
        for part in range(2):
            turned[part, at * LANES : (at + 1) * LANES, :] = tiles[at, pl.ds(part, half, stride=2), :].T
    for block in range(states // half):
        start = (block // 2) * 2 * half + block % 2
        for part in range(2):
            piece = turned[part, pl.ds(start, half, stride=2), :]
            at = block * half % depth
            parts[block * half // depth][at : at + half, part * half : (part + 1) * half] = piece


def gather_kernel(flips, share, depth, *refs):
    _, spot, row = place()
    near, far, rest = refs[: len(flips)], refs[len(flips) : 2 * len(flips)], refs[2 * len(flips) :]
    high_ref, low_ref = rest[-2 - (share > 0)], rest[-1 - (share > 0)]
    for index, flip in enumerate(flips):
        at = jnp.bitwise_xor(spot, flip)
        for ref, block in ((near[index], row), (far[index], 1 - row)):
            high, low = split(ref[0:depth, :])
            high_ref[at, block] = high
            low_ref[at, block] = low
    if share:
        rest[-1][spot] = rest[0][...]
        for flip in range(1, GROUP):
            rest[-1][jnp.bitwise_xor(spot, flip)] = near[flip][depth : depth + share, :]


def choose_kernel(first_ref, second_ref, out_ref):
    _, _, row = place()

    @pl.when(row == 0)
    def _():
        out_ref[...] = first_ref[...]

    @pl.when(row != 0)
    def _():
        out_ref[...] = second_ref[...]


def pack(spot, step, refs, state):
    for flip, ref in enumerate(refs):

        @pl.when(spot == (step ^ flip))
        def _():
            ref[...] = state


def filter_steps(state, coef_ref, high_ref, low_ref, obs_ref, keep):
    half = high_ref.shape[3] // 2
    for step in range(GROUP):
        moved, values = transition(state, coef_ref, half)
        innovation = -values if obs_ref is None else obs_ref[step] - values
        update = [
            multiply(innovation, high_ref[step, block], low_ref[step, block]) for block in range(high_ref.shape[1])
        ]
        state = moved + jnp.concatenate(update, 1)
        keep(step, state)
    return state


def filter_kernel(turn, middle, start_ref, coef_ref, high_ref, low_ref, obs_ref, *rest):
    lasts = () if middle else rest[-1:]
    outs = rest[-GROUP - 1 :] if middle else rest[-GROUP - 2 : -1]
    out_ref, sent = outs[0], outs[1:]
    group, spot, _ = place()

    @pl.when(group == turn)
    def _():
        def keep(step, state):
            out_ref[step] = state
            pack(spot, step, sent, state)

        state = filter_steps(start_ref[...], coef_ref, high_ref, low_ref, obs_ref, keep)
        for ref in lasts:
            ref[...] = state


def joined_filter_kernel(groups, coef_ref, high_ref, low_ref, obs_ref, map_high_ref, map_low_ref, offset_ref):
    group, _, _ = place()

    @pl.when(jnp.logical_and(group > 0, group < groups - 1))
    def _():
        blocks, states, lanes = map_high_ref.shape
        nothing = jnp.zeros(offset_ref.shape, F32)
        offset_ref[...] = filter_steps(nothing, coef_ref, high_ref, low_ref, obs_ref, lambda *_: None)
        rows = lax.broadcasted_iota(jnp.int32, (states, states), 0)
        columns = lax.broadcasted_iota(jnp.int32, (states, states), 1)
        unit = jnp.where(rows == columns, 1.0, 0.0)
        joined = filter_steps(unit, coef_ref, high_ref, low_ref, None, lambda *_: None)
        for block in range(blocks):
            part = joined[:, block * lanes : (block + 1) * lanes]
            map_high_ref[block], map_low_ref[block] = split(part)


def smooth_steps(state, coef_ref, high_ref, low_ref, filt_ref, keep, last_group=False):
    half = high_ref.shape[3] // 2
    for step in range(GROUP - 1, -1, -1):
        filt = filt_ref[step]
        if last_group and step == GROUP - 1:
            state = filt
        else:
            change = state - transition(filt, coef_ref, half)[0]
            update = [
                multiply(change, high_ref[step, block], low_ref[step, block]) for block in range(high_ref.shape[1])
            ]
            state = filt + jnp.concatenate(update, 1)
        keep(step, state)
    return state


def smooth_kernel(turn, groups, start_ref, coef_ref, high_ref, low_ref, filt_ref, *rest):
    sent, first = (rest[-GROUP - 1 : -1], rest[-1:]) if turn == 0 else (rest[-GROUP:], ())
    group, spot, _ = place()

    @pl.when(group == groups - 1 - turn)
    def _():
        keep = lambda step, state: pack(spot, step, sent, state)
        state = smooth_steps(start_ref[...], coef_ref, high_ref, low_ref, filt_ref, keep, turn == 0)
        for ref in first:
            ref[...] = state


def joined_kernel(groups, coef_ref, high_ref, low_ref, filt_ref, map_high_ref, map_low_ref, offset_ref):
    group, _, _ = place()

    @pl.when(jnp.logical_and(group > 0, group < groups - 1))
    def _():
        blocks, lanes = high_ref.shape[1], high_ref.shape[3]
        nothing = jnp.zeros(offset_ref.shape, F32)
        offset_ref[...] = smooth_steps(nothing, coef_ref, high_ref, low_ref, filt_ref, lambda *_: None)
        last = GROUP - 1
        joined = [high_ref[last, block].astype(F32) + low_ref[last, block].astype(F32) for block in range(blocks)]
        for step in range(GROUP - 2, -1, -1):
            whole = jnp.concatenate(joined, 1)
            joined = [multiply(whole, high_ref[step, block], low_ref[step, block]) for block in range(blocks)]
        for block in range(blocks):
            map_high_ref[block], map_low_ref[block] = split(joined[block])


def jump_kernel(active, start_ref, map_high_ref, map_low_ref, offset_ref, first_ref):
    group, _, _ = place()

    @pl.when(group == active)
    def _():
        start = start_ref[...]
        moved = [multiply(start, map_high_ref[block], map_low_ref[block]) for block in range(map_high_ref.shape[0])]
        first_ref[...] = offset_ref[...] + jnp.concatenate(moved, 1)


def across_kernel(slots, *refs):
    _, _, row = place()
    lanes = refs[-1].shape[2]
    for slot, ref in zip(slots, refs):
        refs[-1][slot] = ref[:, pl.ds(pl.multiple_of((1 - row) * lanes, LANES), lanes)]


def home_kernel(share, *refs):
    near, (far_ref, *outs, turned, tiles) = refs[: 2 * GROUP], refs[2 * GROUP :]
    _, spot, row = place()
    rows = lax.axis_size("rows")
    panel, paths = outs[0].shape
    half = panel // 2
    lanes = pl.ds(pl.multiple_of(row * panel, LANES), panel)
    for kind, out_ref in enumerate(outs):
        for flip in range(GROUP):
            at = kind * GROUP + flip
            start = jnp.bitwise_xor(spot, flip) * rows
            turned[kind, pl.ds(pl.multiple_of((start + row) * share, 8), share), :] = near[at][:, lanes]
            turned[kind, pl.ds(pl.multiple_of((start + 1 - row) * share, 8), share), :] = far_ref[at]
        for at in range(paths // LANES):
            lines = slice(at * LANES, (at + 1) * LANES)
            for part in range(2):
                piece = turned[kind, lines, part * half : (part + 1) * half].T
                tiles[kind, at, pl.ds(part, half, stride=2), :] = piece
            out_ref[:, lines] = tiles[kind, at]


def gate(values, token, flops):
    return call(
        lambda *refs: None,
        (*values, token),
        [(value.shape, value.dtype) for value in values],
        aliases={at: at for at in range(len(values))},
        flops=flops,
    )


def body(site_rates, prior_mean, observed, obs_mask, filter_gains, smooth_gains):
    count, rows = lax.axis_size("tm"), lax.axis_size("rows")
    groups = count // GROUP
    panel, sites = filter_gains.shape[1:]
    states, paths = prior_mean.shape
    half = panel // 2
    share = paths // (GROUP * rows)
    both = ("tm", "rows")

    def swap(value, target):
        pairs = [(t * rows + r, target(t, r)) for t in range(count) for r in range(rows)]
        return lax.ppermute(value, both, pairs)

    def across(value, flip):
        return swap(value, lambda t, r: (t ^ flip) * rows + r)

    def forward(value):
        return swap(value, lambda t, r: (t ^ (2 - r)) * rows + r)

    def neighbour(value):
        return swap(value, lambda t, r: t * rows + 1 - r)

    def hop(value, source, target):
        pairs = [
            ((source * GROUP + m) * rows + r, (target * GROUP + m) * rows + r)
            for m in range(GROUP)
            for r in range(rows)
        ]
        return lax.ppermute(value, both, pairs)

    def send_home(sent):
        return [across(sent[flip], flip) for flip in reversed(range(1, GROUP))][::-1]

    *messages, own_obs, coef = call(
        functools.partial(gain_kernel, share),
        tuple(pltpu.with_memory_space_constraint(x, pltpu.HBM) for x in (site_rates.reshape(1, sites), obs_mask, filter_gains[0], observed[0])),
        [((sites + share, panel), F32)] * (GROUP - 1) + [((share, sites), F32), ((8, sites), F32)],
        [
            pltpu.VMEM((1, sites), F32),
            pltpu.VMEM((1, sites), jnp.int32),
            pltpu.VMEM((panel, sites), F32),
            pltpu.VMEM((sites, paths), F32),
            pltpu.VMEM((paths, sites), F32),
            pltpu.VMEM((sites // LANES, panel, LANES), F32),
            pltpu.SemaphoreType.DMA((4,)),
        ],
        source=pltpu.HBM,
    )
    near = [across(value, flip) for flip, value in enumerate(messages, 1)]
    (prior,) = call(
        functools.partial(prior_kernel, share, half),
        (prior_mean,),
        [((share, states), F32)],
        [pltpu.VMEM((paths, states), F32), pltpu.VMEM((paths // LANES, states, LANES), F32)],
    )
    pieces = call(
        smoother_gain_kernel,
        (smooth_gains[0],),
        [((states // PIECES, panel), F32)] * PIECES,
        [pltpu.VMEM((2, states, half), F32), pltpu.VMEM((states // LANES, panel, LANES), F32)],
    )
    (turned_gain,) = pieces
    gain_x, gain_y = across(turned_gain, 1), across(turned_gain, 2)
    own_far, prior = lax.optimization_barrier((neighbour(messages[0]), prior))
    *near, own_far, prior, turned_gain = lax.optimization_barrier((*near, own_far, prior, turned_gain))
    far = [own_far] + [neighbour(value) for value in near]
    near = [messages[0], *near]
    high, low, obs = call(
        functools.partial(gather_kernel, range(GROUP), share, sites),
        (*near, *far, own_obs),
        [((GROUP, rows, sites, panel), BF16)] * 2 + [((GROUP, share, sites), F32)],
    )
    start, filtered = prior, ()
    *joined, offset = call(
        functools.partial(joined_filter_kernel, groups),
        (coef, high, low, obs),
        [((rows, states, panel), BF16)] * 2 + [((share, states), F32)],
        flops=JP,
    )
    for turn in range(groups):
        middle = 0 < turn < groups - 1
        if middle:
            (last,) = call(
                functools.partial(jump_kernel, turn), (start, *joined, offset), [((share, states), F32)], flops=JJ
            )
            there = hop(last, turn, turn + 1)
        filtered = call(
            functools.partial(filter_kernel, turn, middle),
            (start, coef, high, low, obs, *filtered),
            [((GROUP, share, states), F32)] + [((share, states), F32)] * (GROUP + 1 - middle),
            aliases={5 + i: i for i in range(len(filtered))},
            flops=FW[min(turn,3)],
        )
        if not middle:
            *filtered, last = filtered
        if turn == 0:
            there = hop(last, 0, 1)
        if turn < groups - 1:
            start = there
        if turn == groups - 3:
            turned_gain, gain_x, gain_y = gate((turned_gain, gain_x, gain_y), last, G1)
            (gain_d,) = call(choose_kernel, (gain_x, gain_y), [((states, panel), F32)], flops=G1)
            gain_d = forward(gain_d)
            gain_near = list(gate((turned_gain, gain_x, gain_y), start, G2))
            gain_far = [neighbour(value) for value in gain_near]
        if turn == groups - 2:
            parts = call(
                functools.partial(gather_kernel, range(GROUP - 1), 0, states),
                (*gain_near, *gain_far),
                [((GROUP, rows, states, panel), BF16)] * 2,
                flops=GA,
            )
            (gain_d,) = gate((gain_d,), parts[0], G3)
            high_back, low_back = call(
                functools.partial(gather_kernel, (GROUP - 1,), 0, states),
                (gain_d, neighbour(gain_d), *parts),
                [((GROUP, rows, states, panel), BF16)] * 2,
                aliases={2: 0, 3: 1},
            )
    filtered, sent = filtered[0], filtered[1:]

    high, low = high_back, low_back
    start, packed = last, ()
    *joined, offset = call(
        functools.partial(joined_kernel, groups),
        (coef, high, low, filtered),
        [((rows, states, panel), BF16)] * 2 + [((share, states), F32)],
        flops=JF,
    )
    for turn in range(groups):
        middle = 0 < turn < groups - 1
        if middle:
            (first,) = call(
                functools.partial(jump_kernel, groups - 1 - turn), (start, *joined, offset), [((share, states), F32)]
            )
            here = hop(first, groups - 1 - turn, groups - 2 - turn)
        packed = call(
            functools.partial(smooth_kernel, turn, groups),
            (start, coef, high, low, filtered, *packed),
            [((share, states), F32)] * (GROUP + (turn == 0)),
            aliases={5 + i: i for i in range(len(packed))},
            flops=BW[1] if middle else BW[0],
        )
        if turn == 0:
            *packed, first = packed
            here = hop(first, groups - 1, groups - 2)
        if turn == groups - 2:
            sent = gate(sent, first, G4)
            sent = [sent[0], *send_home(sent)]
        if turn < groups - 1:
            start = here
    near = (*sent, packed[0], *send_home(packed))
    early = (*range(GROUP + 1), 2 * GROUP - 1)
    late = [slot for slot in range(2 * GROUP) if slot not in early]
    far_shape = [((2 * GROUP, share, panel), F32)]
    far = call(functools.partial(across_kernel, early), [near[slot] for slot in early], far_shape)
    (far,) = call(
        functools.partial(across_kernel, late),
        (*[near[slot] for slot in late], *far),
        far_shape,
        aliases={len(late): 0},
        flops=AF,
    )
    filt, smooth = call(
        functools.partial(home_kernel, share),
        (*near, neighbour(far)),
        [((panel, paths), F32)] * 2,
        [pltpu.VMEM((2, paths, panel), F32), pltpu.VMEM((2, paths // LANES, panel, LANES), F32)],
    )
    return filt[None], smooth[None]


def solution(mesh):
    placed = (
        P(),
        P(),
        P("tm", None, None),
        P("tm", None),
        P("tm", "rows", None),
        P("tm", "rows", None),
    )
    return jax.shard_map(
        body,
        mesh=mesh,
        in_specs=placed,
        out_specs=(P("tm", "rows", None), P("tm", "rows", None)),
        check_vma=False,
    )
```

```python
import functools

import jax
import jax.numpy as jnp
from jax import lax
from jax.experimental import pallas as pl
from jax.experimental.pallas import tpu as pltpu
from jax.sharding import PartitionSpec as P

GROUP = 4
LANES = 128
PIECES = 1
FW = (0, 0, 10**11, 10**11)
BW = (0, 10**10)
JF = 10**11
JP = 0
JJ = 0
GA = 10**10
AF = 0
G1 = G2 = G3 = 10**9
G4 = 10**9
G6 = 10**9
G5 = 10**10
BF16 = jnp.bfloat16
F32 = jnp.float32


def call(kernel, operands, shapes, scratch=(), aliases=None, source=pltpu.VMEM, bytes_accessed=2 << 20, flops=0, grant=24 << 20):
    return pl.pallas_call(
        kernel,
        out_shape=[jax.ShapeDtypeStruct(shape, dtype) for shape, dtype in shapes],
        in_specs=[pl.BlockSpec(memory_space=source)] * len(operands),
        out_specs=[pl.BlockSpec(memory_space=pltpu.VMEM)] * len(shapes),
        scratch_shapes=list(scratch),
        input_output_aliases=aliases or {},
        compiler_params=pltpu.CompilerParams(vmem_limit_bytes=grant),
        cost_estimate=pl.CostEstimate(flops=flops, bytes_accessed=bytes_accessed, transcendentals=0),
    )(*operands)


def place():
    step = lax.axis_index("tm")
    return lax.div(step, GROUP), lax.rem(step, GROUP), lax.axis_index("rows")


def split(value):
    high = value.astype(BF16)
    return high, (value - high.astype(F32)).astype(BF16)


def multiply(value, high_ref, low_ref):
    high, low = split(value)
    count = value.shape[0]
    both = jnp.dot(jnp.concatenate([high, low], 0), high_ref, preferred_element_type=F32)
    return both[:count] + both[count:] + jnp.dot(high, low_ref, preferred_element_type=F32)


def transition(state, coef_ref, half):
    values, slopes = [], []
    for block in range(state.shape[1] // (2 * half)):
        at = 2 * half * block
        value, slope = state[:, at : at + half], state[:, at + half : at + 2 * half]
        lanes = slice(block * half, (block + 1) * half)
        values.append(coef_ref[0:1, lanes] * value + coef_ref[1:2, lanes] * slope)
        slopes.append(coef_ref[2:3, lanes] * value + coef_ref[3:4, lanes] * slope)
    moved = jnp.concatenate([part for pair in zip(values, slopes) for part in pair], 1)
    return moved, jnp.concatenate(values, 1)


def lane_tiles(value):
    return [value[:, at : at + LANES] for at in range(0, value.shape[1], LANES)]


def fetch(source, target, sem):
    copy = pltpu.make_async_copy(source, target, sem)
    copy.start()
    return copy


def gain_kernel(
    share,
    rates_hbm,
    mask_hbm,
    gain_hbm,
    obs_hbm,
    first_ref,
    second_ref,
    third_ref,
    own_ref,
    coef_ref,
    rates_ref,
    mask_ref,
    gain_ref,
    obs_ref,
    turned,
    tiles,
    sems,
):
    sent = (first_ref, second_ref, third_ref)
    copies = [
        fetch(source, target, sems.at[at])
        for at, (source, target) in enumerate(
            ((mask_hbm, mask_ref), (gain_hbm, gain_ref), (obs_hbm, obs_ref), (rates_hbm, rates_ref))
        )
    ]
    _, spot, row = place()
    panel, sites = gain_ref.shape
    half = panel // 2
    copies[0].wait()
    copies[1].wait()
    mask = mask_ref[...].astype(F32)
    for at, tile in enumerate(lane_tiles(gain_ref[...] * mask)):
        tiles[at] = tile
        lines = slice(at * LANES, (at + 1) * LANES)
        for part in range(2):
            piece = tiles[at, pl.ds(part, half, stride=2), :].T
            lanes = slice(part * half, (part + 1) * half)
            for ref in sent:
                ref[lines, lanes] = piece
    copies[2].wait()
    turned[...] = obs_ref[...].T
    rows = lax.axis_size("rows")

    def slice_for(flip):
        start = (jnp.bitwise_xor(spot, flip) * rows + row) * share
        return turned[pl.ds(pl.multiple_of(start, 8), share), :]

    for flip, ref in enumerate(sent, 1):
        ref[sites : sites + share, :] = slice_for(flip)
    own_ref[...] = slice_for(0)
    copies[3].wait()
    rate = rates_ref[...]
    decay = jnp.exp(-rate)
    coef_ref[0:1, :] = decay * (1.0 + rate)
    coef_ref[1:2, :] = decay
    coef_ref[2:3, :] = -decay * rate * rate
    coef_ref[3:4, :] = decay * (1.0 - rate)
    coef_ref[4:8, :] = jnp.zeros((4, sites), F32)


def prior_kernel(share, half, prior_ref, out_ref, turned, tiles):
    _, spot, row = place()
    rows = lax.axis_size("rows")
    for at, tile in enumerate(lane_tiles(prior_ref[...])):
        tiles[at] = tile
        for block in range(prior_ref.shape[0] // half):
            start = (block // 2) * 2 * half + block % 2
            piece = tiles[at, pl.ds(start, half, stride=2), :].T
            turned[at * LANES : (at + 1) * LANES, block * half : (block + 1) * half] = piece
    start = (spot * rows + row) * share
    out_ref[...] = turned[pl.ds(pl.multiple_of(start, 8), share), :]


def smoother_gain_kernel(gain_ref, *refs):
    parts, (turned, tiles) = refs[:-2], refs[-2:]
    depth = parts[0].shape[0]
    panel, states = gain_ref.shape
    half = panel // 2
    for at, tile in enumerate(lane_tiles(gain_ref[...])):
        tiles[at] = tile
        for part in range(2):
            turned[part, at * LANES : (at + 1) * LANES, :] = tiles[at, pl.ds(part, half, stride=2), :].T
    for block in range(states // half):
        start = (block // 2) * 2 * half + block % 2
        for part in range(2):
            piece = turned[part, pl.ds(start, half, stride=2), :]
            at = block * half % depth
            parts[block * half // depth][at : at + half, part * half : (part + 1) * half] = piece


def gather_kernel(flips, share, depth, *refs):
    _, spot, row = place()
    near, far, rest = refs[: len(flips)], refs[len(flips) : 2 * len(flips)], refs[2 * len(flips) :]
    high_ref, low_ref = rest[-2 - (share > 0)], rest[-1 - (share > 0)]
    for index, flip in enumerate(flips):
        at = jnp.bitwise_xor(spot, flip)
        for ref, block in ((near[index], row), (far[index], 1 - row)):
            high, low = split(ref[0:depth, :])
            high_ref[at, block] = high
            low_ref[at, block] = low
    if share:
        rest[-1][spot] = rest[0][...]
        for flip in range(1, GROUP):
            rest[-1][jnp.bitwise_xor(spot, flip)] = near[flip][depth : depth + share, :]


def choose_kernel(first_ref, second_ref, out_ref):
    _, _, row = place()

    @pl.when(row == 0)
    def _():
        out_ref[...] = first_ref[...]

    @pl.when(row != 0)
    def _():
        out_ref[...] = second_ref[...]


def pack(spot, step, refs, state):
    for flip, ref in enumerate(refs):

        @pl.when(spot == (step ^ flip))
        def _():
            ref[...] = state


def filter_steps(state, coef_ref, high_ref, low_ref, obs_ref, keep):
    half = high_ref.shape[3] // 2
    for step in range(GROUP):
        moved, values = transition(state, coef_ref, half)
        innovation = -values if obs_ref is None else obs_ref[step] - values
        update = [
            multiply(innovation, high_ref[step, block], low_ref[step, block]) for block in range(high_ref.shape[1])
        ]
        state = moved + jnp.concatenate(update, 1)
        keep(step, state)
    return state


def filter_kernel(turn, middle, start_ref, coef_ref, high_ref, low_ref, obs_ref, *rest):
    lasts = () if middle else rest[-1:]
    outs = rest[-GROUP - 1 :] if middle else rest[-GROUP - 2 : -1]
    out_ref, sent = outs[0], outs[1:]
    group, spot, _ = place()

    @pl.when(group == turn)
    def _():
        def keep(step, state):
            out_ref[step] = state
            pack(spot, step, sent, state)

        state = filter_steps(start_ref[...], coef_ref, high_ref, low_ref, obs_ref, keep)
        for ref in lasts:
            ref[...] = state


def joined_filter_kernel(groups, coef_ref, high_ref, low_ref, obs_ref, map_high_ref, map_low_ref, offset_ref):
    group, _, _ = place()

    @pl.when(jnp.logical_and(group > 0, group < groups - 1))
    def _():
        blocks, states, lanes = map_high_ref.shape
        nothing = jnp.zeros(offset_ref.shape, F32)
        offset_ref[...] = filter_steps(nothing, coef_ref, high_ref, low_ref, obs_ref, lambda *_: None)
        rows = lax.broadcasted_iota(jnp.int32, (states, states), 0)
        columns = lax.broadcasted_iota(jnp.int32, (states, states), 1)
        unit = jnp.where(rows == columns, 1.0, 0.0)
        joined = filter_steps(unit, coef_ref, high_ref, low_ref, None, lambda *_: None)
        for block in range(blocks):
            part = joined[:, block * lanes : (block + 1) * lanes]
            map_high_ref[block], map_low_ref[block] = split(part)


def smooth_steps(state, coef_ref, high_ref, low_ref, filt_ref, keep, last_group=False):
    half = high_ref.shape[3] // 2
    for step in range(GROUP - 1, -1, -1):
        filt = filt_ref[step]
        if last_group and step == GROUP - 1:
            state = filt
        else:
            change = state - transition(filt, coef_ref, half)[0]
            update = [
                multiply(change, high_ref[step, block], low_ref[step, block]) for block in range(high_ref.shape[1])
            ]
            state = filt + jnp.concatenate(update, 1)
        keep(step, state)
    return state


def smooth_kernel(turn, groups, start_ref, coef_ref, high_ref, low_ref, filt_ref, *rest):
    sent, first = (rest[-GROUP - 1 : -1], rest[-1:]) if turn == 0 else (rest[-GROUP:], ())
    group, spot, _ = place()

    @pl.when(group == groups - 1 - turn)
    def _():
        keep = lambda step, state: pack(spot, step, sent, state)
        state = smooth_steps(start_ref[...], coef_ref, high_ref, low_ref, filt_ref, keep, turn == 0)
        for ref in first:
            ref[...] = state


def joined_kernel(groups, coef_ref, high_ref, low_ref, filt_ref, map_high_ref, map_low_ref, offset_ref):
    group, _, _ = place()

    @pl.when(jnp.logical_and(group > 0, group < groups - 1))
    def _():
        blocks, lanes = high_ref.shape[1], high_ref.shape[3]
        nothing = jnp.zeros(offset_ref.shape, F32)
        offset_ref[...] = smooth_steps(nothing, coef_ref, high_ref, low_ref, filt_ref, lambda *_: None)
        last = GROUP - 1
        joined = [high_ref[last, block].astype(F32) + low_ref[last, block].astype(F32) for block in range(blocks)]
        for step in range(GROUP - 2, -1, -1):
            whole = jnp.concatenate(joined, 1)
            joined = [multiply(whole, high_ref[step, block], low_ref[step, block]) for block in range(blocks)]
        for block in range(blocks):
            map_high_ref[block], map_low_ref[block] = split(joined[block])


def jump_kernel(active, start_ref, map_high_ref, map_low_ref, offset_ref, first_ref):
    group, _, _ = place()

    @pl.when(group == active)
    def _():
        start = start_ref[...]
        moved = [multiply(start, map_high_ref[block], map_low_ref[block]) for block in range(map_high_ref.shape[0])]
        first_ref[...] = offset_ref[...] + jnp.concatenate(moved, 1)


def across_kernel(slots, *refs):
    _, _, row = place()
    lanes = refs[-1].shape[2]
    for slot, ref in zip(slots, refs):
        refs[-1][slot] = ref[:, pl.ds(pl.multiple_of((1 - row) * lanes, LANES), lanes)]


def home_kernel(share, *refs):
    near, (*fars, filt_ref, smooth_ref, turned, tiles) = refs[: 2 * GROUP], refs[2 * GROUP :]
    outs = (filt_ref, smooth_ref)
    _, spot, row = place()
    rows = lax.axis_size("rows")
    panel, paths = outs[0].shape
    half = panel // 2
    lanes = pl.ds(pl.multiple_of(row * panel, LANES), panel)
    for kind, out_ref in enumerate(outs):
        for flip in range(GROUP):
            at = kind * GROUP + flip
            start = jnp.bitwise_xor(spot, flip) * rows
            turned[kind, pl.ds(pl.multiple_of((start + row) * share, 8), share), :] = near[at][:, lanes]
            turned[kind, pl.ds(pl.multiple_of((start + 1 - row) * share, 8), share), :] = fars[kind][flip]
        for at in range(paths // LANES):
            lines = slice(at * LANES, (at + 1) * LANES)
            for part in range(2):
                piece = turned[kind, lines, part * half : (part + 1) * half].T
                tiles[kind, at, pl.ds(part, half, stride=2), :] = piece
            out_ref[:, lines] = tiles[kind, at]


def gate(values, token, flops):
    return call(
        lambda *refs: None,
        (*values, token),
        [(value.shape, value.dtype) for value in values],
        aliases={at: at for at in range(len(values))},
        flops=flops,
    )


def body(site_rates, prior_mean, observed, obs_mask, filter_gains, smooth_gains):
    count, rows = lax.axis_size("tm"), lax.axis_size("rows")
    groups = count // GROUP
    panel, sites = filter_gains.shape[1:]
    states, paths = prior_mean.shape
    half = panel // 2
    share = paths // (GROUP * rows)
    both = ("tm", "rows")

    def swap(value, target):
        pairs = [(t * rows + r, target(t, r)) for t in range(count) for r in range(rows)]
        return lax.ppermute(value, both, pairs)

    def across(value, flip):
        return swap(value, lambda t, r: (t ^ flip) * rows + r)

    def forward(value):
        return swap(value, lambda t, r: (t ^ (2 - r)) * rows + r)

    def neighbour(value):
        return swap(value, lambda t, r: t * rows + 1 - r)

    def hop(value, source, target):
        pairs = [
            ((source * GROUP + m) * rows + r, (target * GROUP + m) * rows + r)
            for m in range(GROUP)
            for r in range(rows)
        ]
        return lax.ppermute(value, both, pairs)

    def send_home(sent):
        return [across(sent[flip], flip) for flip in reversed(range(1, GROUP))][::-1]

    *messages, own_obs, coef = call(
        functools.partial(gain_kernel, share),
        tuple(pltpu.with_memory_space_constraint(x, pltpu.HBM) for x in (site_rates.reshape(1, sites), obs_mask, filter_gains[0], observed[0])),
        [((sites + share, panel), F32)] * (GROUP - 1) + [((share, sites), F32), ((8, sites), F32)],
        [
            pltpu.VMEM((1, sites), F32),
            pltpu.VMEM((1, sites), jnp.int32),
            pltpu.VMEM((panel, sites), F32),
            pltpu.VMEM((sites, paths), F32),
            pltpu.VMEM((paths, sites), F32),
            pltpu.VMEM((sites // LANES, panel, LANES), F32),
            pltpu.SemaphoreType.DMA((4,)),
        ],
        source=pltpu.HBM,
    )
    near = [across(value, flip) for flip, value in enumerate(messages, 1)]
    (prior,) = call(
        functools.partial(prior_kernel, share, half),
        (prior_mean,),
        [((share, states), F32)],
        [pltpu.VMEM((paths, states), F32), pltpu.VMEM((paths // LANES, states, LANES), F32)],
    )
    pieces = call(
        smoother_gain_kernel,
        (smooth_gains[0],),
        [((states // PIECES, panel), F32)] * PIECES,
        [pltpu.VMEM((2, states, half), F32), pltpu.VMEM((states // LANES, panel, LANES), F32)],
    )
    (turned_gain,) = pieces
    gain_x, gain_y = across(turned_gain, 1), across(turned_gain, 2)
    own_far, prior = lax.optimization_barrier((neighbour(messages[0]), prior))
    *near, own_far, prior, turned_gain = lax.optimization_barrier((*near, own_far, prior, turned_gain))
    far = [own_far] + [neighbour(value) for value in near]
    near = [messages[0], *near]
    high, low, obs = call(
        functools.partial(gather_kernel, range(GROUP), share, sites),
        (*near, *far, own_obs),
        [((GROUP, rows, sites, panel), BF16)] * 2 + [((GROUP, share, sites), F32)],
    )
    start, filtered = prior, ()
    *joined, offset = call(
        functools.partial(joined_filter_kernel, groups),
        (coef, high, low, obs),
        [((rows, states, panel), BF16)] * 2 + [((share, states), F32)],
        flops=JP,
    )
    for turn in range(groups):
        middle = 0 < turn < groups - 1
        if middle:
            (last,) = call(
                functools.partial(jump_kernel, turn), (start, *joined, offset), [((share, states), F32)], flops=JJ
            )
            there = hop(last, turn, turn + 1)
        filtered = call(
            functools.partial(filter_kernel, turn, middle),
            (start, coef, high, low, obs, *filtered),
            [((GROUP, share, states), F32)] + [((share, states), F32)] * (GROUP + 1 - middle),
            aliases={5 + i: i for i in range(len(filtered))},
            flops=FW[min(turn,3)],
        )
        if not middle:
            *filtered, last = filtered
        if turn == 0:
            there = hop(last, 0, 1)
        if turn < groups - 1:
            start = there
        if turn == groups - 3:
            turned_gain, gain_x, gain_y = gate((turned_gain, gain_x, gain_y), last, G1)
            (gain_d,) = call(choose_kernel, (gain_x, gain_y), [((states, panel), F32)], flops=G1)
            gain_d = forward(gain_d)
            gain_near = list(gate((turned_gain, gain_x, gain_y), start, G2))
            gain_far = [neighbour(value) for value in gain_near]
        if turn == groups - 2:
            parts = call(
                functools.partial(gather_kernel, range(GROUP - 1), 0, states),
                (*gain_near, *gain_far),
                [((GROUP, rows, states, panel), BF16)] * 2,
                flops=GA,
            )
            (gain_d,) = gate((gain_d,), parts[0], G3)
            high_back, low_back = call(
                functools.partial(gather_kernel, (GROUP - 1,), 0, states),
                (gain_d, neighbour(gain_d), *parts),
                [((GROUP, rows, states, panel), BF16)] * 2,
                aliases={2: 0, 3: 1},
            )
    filtered, sent = filtered[0], filtered[1:]

    high, low = high_back, low_back
    start, packed = last, ()
    *joined, offset = call(
        functools.partial(joined_kernel, groups),
        (coef, high, low, filtered),
        [((rows, states, panel), BF16)] * 2 + [((share, states), F32)],
        flops=JF,
    )
    for turn in range(groups):
        middle = 0 < turn < groups - 1
        if middle:
            (first,) = call(
                functools.partial(jump_kernel, groups - 1 - turn), (start, *joined, offset), [((share, states), F32)]
            )
            here = hop(first, groups - 1 - turn, groups - 2 - turn)
        packed = call(
            functools.partial(smooth_kernel, turn, groups),
            (start, coef, high, low, filtered, *packed),
            [((share, states), F32)] * (GROUP + (turn == 0)),
            aliases={5 + i: i for i in range(len(packed))},
            flops=BW[1] if middle else BW[0],
        )
        if turn == 0:
            *packed, first = packed
            here = hop(first, groups - 1, groups - 2)
        if turn == groups - 2:
            sent = gate(sent, first, G4)
            sent = [sent[0], *send_home(sent)]
        if turn < groups - 1:
            start = here
    far_shape = [((GROUP, share, panel), F32)]
    smooth_near = (packed[0], *send_home(packed))
    (filt_far,) = call(functools.partial(across_kernel, range(GROUP)), sent, far_shape)
    early = (0, GROUP - 1)
    late = range(1, GROUP - 1)
    far = call(functools.partial(across_kernel, early), [smooth_near[slot] for slot in early], far_shape)
    (far,) = call(
        functools.partial(across_kernel, late),
        (*[smooth_near[slot] for slot in late], *far),
        far_shape,
        aliases={len(late): 0},
    )
    filt, smooth = call(
        functools.partial(home_kernel, share),
        (*sent, *smooth_near, neighbour(filt_far), neighbour(far)),
        [((panel, paths), F32)] * 2,
        [pltpu.VMEM((2, paths, panel), F32), pltpu.VMEM((2, paths // LANES, panel, LANES), F32)],
    )
    return filt[None], smooth[None]


def solution(mesh):
    placed = (
        P(),
        P(),
        P("tm", None, None),
        P("tm", None),
        P("tm", "rows", None),
        P("tm", "rows", None),
    )
    return jax.shard_map(
        body,
        mesh=mesh,
        in_specs=placed,
        out_specs=(P("tm", "rows", None), P("tm", "rows", None)),
        check_vma=False,
    )
```

```python
import functools

import jax
import jax.numpy as jnp
from jax import lax
from jax.experimental import pallas as pl
from jax.experimental.pallas import tpu as pltpu
from jax.sharding import PartitionSpec as P

GROUP = 4
LANES = 128
SPARE = 8
FW = (0, 0, 10**11, 10**11)
BW = (0, 10**10)
JF = 10**11
JP = 0
JJ = 0
GA = 10**10
G1 = G2 = G3 = 10**9
G4 = 10**9
BF16 = jnp.bfloat16
F32 = jnp.float32


def call(kernel, operands, shapes, scratch=(), aliases=None, source=pltpu.VMEM, bytes_accessed=2 << 20, flops=0, grant=24 << 20):
    return pl.pallas_call(
        kernel,
        out_shape=[jax.ShapeDtypeStruct(shape, dtype) for shape, dtype in shapes],
        in_specs=[pl.BlockSpec(memory_space=source)] * len(operands),
        out_specs=[pl.BlockSpec(memory_space=pltpu.VMEM)] * len(shapes),
        scratch_shapes=list(scratch),
        input_output_aliases=aliases or {},
        compiler_params=pltpu.CompilerParams(vmem_limit_bytes=grant),
        cost_estimate=pl.CostEstimate(flops=flops, bytes_accessed=bytes_accessed, transcendentals=0),
    )(*operands)


def place():
    step = lax.axis_index("tm")
    return lax.div(step, GROUP), lax.rem(step, GROUP), lax.axis_index("rows")


def split(value):
    high = value.astype(BF16)
    return high, (value - high.astype(F32)).astype(BF16)


def multiply(value, high_ref, low_ref):
    high, low = split(value)
    count = value.shape[0]
    both = jnp.dot(jnp.concatenate([high, low], 0), high_ref, preferred_element_type=F32)
    return both[:count] + both[count:] + jnp.dot(high, low_ref, preferred_element_type=F32)


def transition(state, coef_ref, half):
    values, slopes = [], []
    for block in range(state.shape[1] // (2 * half)):
        at = 2 * half * block
        value, slope = state[:, at : at + half], state[:, at + half : at + 2 * half]
        lanes = slice(block * half, (block + 1) * half)
        values.append(coef_ref[0:1, lanes] * value + coef_ref[1:2, lanes] * slope)
        slopes.append(coef_ref[2:3, lanes] * value + coef_ref[3:4, lanes] * slope)
    moved = jnp.concatenate([part for pair in zip(values, slopes) for part in pair], 1)
    return moved, jnp.concatenate(values, 1)


def lane_tiles(value):
    return [value[:, at : at + LANES] for at in range(0, value.shape[1], LANES)]


def fetch(source, target, sem):
    copy = pltpu.make_async_copy(source, target, sem)
    copy.start()
    return copy


def gain_kernel(
    share,
    rates_hbm,
    mask_hbm,
    gain_hbm,
    obs_hbm,
    first_ref,
    second_ref,
    third_ref,
    own_ref,
    coef_ref,
    rates_ref,
    mask_ref,
    gain_ref,
    obs_ref,
    turned,
    tiles,
    sems,
):
    sent = (first_ref, second_ref, third_ref)
    copies = [
        fetch(source, target, sems.at[at])
        for at, (source, target) in enumerate(
            ((mask_hbm, mask_ref), (gain_hbm, gain_ref), (obs_hbm, obs_ref), (rates_hbm, rates_ref))
        )
    ]
    _, spot, row = place()
    panel, sites = gain_ref.shape
    half = panel // 2
    copies[0].wait()
    copies[1].wait()
    mask = mask_ref[...].astype(F32)
    for at, tile in enumerate(lane_tiles(gain_ref[...] * mask)):
        tiles[at, 0 : tile.shape[0], :] = tile
        lines = slice(at * LANES, (at + 1) * LANES)
        for part in range(2):
            piece = tiles[at, pl.ds(part, half, stride=2), :].T
            lanes = slice(part * half, (part + 1) * half)
            for ref in sent:
                ref[lines, lanes] = piece
    copies[2].wait()
    turned[...] = obs_ref[...].T
    rows = lax.axis_size("rows")

    def slice_for(flip):
        start = (jnp.bitwise_xor(spot, flip) * rows + row) * share
        return turned[pl.ds(pl.multiple_of(start, 8), share), :]

    for flip, ref in enumerate(sent, 1):
        ref[sites : sites + share, :] = slice_for(flip)
    own_ref[...] = slice_for(0)
    copies[3].wait()
    rate = rates_ref[...]
    decay = jnp.exp(-rate)
    coef_ref[0:1, :] = decay * (1.0 + rate)
    coef_ref[1:2, :] = decay
    coef_ref[2:3, :] = -decay * rate * rate
    coef_ref[3:4, :] = decay * (1.0 - rate)
    coef_ref[4:8, :] = jnp.zeros((4, sites), F32)


def prior_kernel(share, half, prior_ref, out_ref, turned, tiles):
    _, spot, row = place()
    rows = lax.axis_size("rows")
    for at, tile in enumerate(lane_tiles(prior_ref[...])):
        tiles[at, 0 : tile.shape[0], :] = tile
        for block in range(prior_ref.shape[0] // half):
            start = (block // 2) * 2 * half + block % 2
            piece = tiles[at, pl.ds(start, half, stride=2), :].T
            turned[at * LANES : (at + 1) * LANES, block * half : (block + 1) * half] = piece
    start = (spot * rows + row) * share
    out_ref[...] = turned[pl.ds(pl.multiple_of(start, 8), share), :]


def smoother_gain_kernel(gain_ref, *refs):
    parts, (turned, tiles) = refs[:-2], refs[-2:]
    depth = parts[0].shape[0]
    panel, states = gain_ref.shape
    half = panel // 2
    for at, tile in enumerate(lane_tiles(gain_ref[...])):
        tiles[at, 0 : tile.shape[0], :] = tile
        for part in range(2):
            turned[part, at * LANES : (at + 1) * LANES, :] = tiles[at, pl.ds(part, half, stride=2), :].T
    for block in range(states // half):
        start = (block // 2) * 2 * half + block % 2
        for part in range(2):
            piece = turned[part, pl.ds(start, half, stride=2), :]
            at = block * half % depth
            parts[block * half // depth][at : at + half, part * half : (part + 1) * half] = piece


def gather_kernel(flips, share, depth, *refs):
    _, spot, row = place()
    near, far, rest = refs[: len(flips)], refs[len(flips) : 2 * len(flips)], refs[2 * len(flips) :]
    high_ref, low_ref = rest[-2 - (share > 0)], rest[-1 - (share > 0)]
    for index, flip in enumerate(flips):
        at = jnp.bitwise_xor(spot, flip)
        for ref, block in ((near[index], row), (far[index], 1 - row)):
            high, low = split(ref[0:depth, :])
            high_ref[at, block] = high
            low_ref[at, block] = low
    if share:
        rest[-1][spot] = rest[0][...]
        for flip in range(1, GROUP):
            rest[-1][jnp.bitwise_xor(spot, flip)] = near[flip][depth : depth + share, :]


def choose_kernel(first_ref, second_ref, out_ref):
    _, _, row = place()

    @pl.when(row == 0)
    def _():
        out_ref[...] = first_ref[...]

    @pl.when(row != 0)
    def _():
        out_ref[...] = second_ref[...]


def pack(spot, step, refs, state):
    for flip, ref in enumerate(refs):

        @pl.when(spot == (step ^ flip))
        def _():
            ref[...] = state


def filter_steps(state, coef_ref, high_ref, low_ref, obs_ref, keep):
    half = high_ref.shape[3] // 2
    for step in range(GROUP):
        moved, values = transition(state, coef_ref, half)
        innovation = -values if obs_ref is None else obs_ref[step] - values
        update = [
            multiply(innovation, high_ref[step, block], low_ref[step, block]) for block in range(high_ref.shape[1])
        ]
        state = moved + jnp.concatenate(update, 1)
        keep(step, state)
    return state


def filter_kernel(turn, middle, start_ref, coef_ref, high_ref, low_ref, obs_ref, *rest):
    lasts = () if middle else rest[-1:]
    outs = rest[-GROUP - 1 :] if middle else rest[-GROUP - 2 : -1]
    out_ref, sent = outs[0], outs[1:]
    group, spot, _ = place()

    @pl.when(group == turn)
    def _():
        def keep(step, state):
            out_ref[step] = state
            pack(spot, step, sent, state)

        state = filter_steps(start_ref[...], coef_ref, high_ref, low_ref, obs_ref, keep)
        for ref in lasts:
            ref[...] = state


def joined_filter_kernel(groups, coef_ref, high_ref, low_ref, obs_ref, map_high_ref, map_low_ref, offset_ref):
    group, _, _ = place()

    @pl.when(jnp.logical_and(group > 0, group < groups - 1))
    def _():
        blocks, states, lanes = map_high_ref.shape
        nothing = jnp.zeros(offset_ref.shape, F32)
        offset_ref[...] = filter_steps(nothing, coef_ref, high_ref, low_ref, obs_ref, lambda *_: None)
        rows = lax.broadcasted_iota(jnp.int32, (states, states), 0)
        columns = lax.broadcasted_iota(jnp.int32, (states, states), 1)
        unit = jnp.where(rows == columns, 1.0, 0.0)
        joined = filter_steps(unit, coef_ref, high_ref, low_ref, None, lambda *_: None)
        for block in range(blocks):
            part = joined[:, block * lanes : (block + 1) * lanes]
            map_high_ref[block], map_low_ref[block] = split(part)


def smooth_steps(state, coef_ref, high_ref, low_ref, filt_ref, keep, last_group=False):
    half = high_ref.shape[3] // 2
    for step in range(GROUP - 1, -1, -1):
        filt = filt_ref[step]
        if last_group and step == GROUP - 1:
            state = filt
        else:
            change = state - transition(filt, coef_ref, half)[0]
            update = [
                multiply(change, high_ref[step, block], low_ref[step, block]) for block in range(high_ref.shape[1])
            ]
            state = filt + jnp.concatenate(update, 1)
        keep(step, state)
    return state


def smooth_kernel(turn, groups, start_ref, coef_ref, high_ref, low_ref, filt_ref, *rest):
    sent, first = (rest[-GROUP - 1 : -1], rest[-1:]) if turn == 0 else (rest[-GROUP:], ())
    group, spot, _ = place()

    @pl.when(group == groups - 1 - turn)
    def _():
        keep = lambda step, state: pack(spot, step, sent, state)
        state = smooth_steps(start_ref[...], coef_ref, high_ref, low_ref, filt_ref, keep, turn == 0)
        for ref in first:
            ref[...] = state


def joined_kernel(groups, coef_ref, high_ref, low_ref, filt_ref, map_high_ref, map_low_ref, offset_ref):
    group, _, _ = place()

    @pl.when(jnp.logical_and(group > 0, group < groups - 1))
    def _():
        blocks, lanes = high_ref.shape[1], high_ref.shape[3]
        nothing = jnp.zeros(offset_ref.shape, F32)
        offset_ref[...] = smooth_steps(nothing, coef_ref, high_ref, low_ref, filt_ref, lambda *_: None)
        last = GROUP - 1
        joined = [high_ref[last, block].astype(F32) + low_ref[last, block].astype(F32) for block in range(blocks)]
        for step in range(GROUP - 2, -1, -1):
            whole = jnp.concatenate(joined, 1)
            joined = [multiply(whole, high_ref[step, block], low_ref[step, block]) for block in range(blocks)]
        for block in range(blocks):
            map_high_ref[block], map_low_ref[block] = split(joined[block])


def jump_kernel(active, start_ref, map_high_ref, map_low_ref, offset_ref, first_ref):
    group, _, _ = place()

    @pl.when(group == active)
    def _():
        start = start_ref[...]
        moved = [multiply(start, map_high_ref[block], map_low_ref[block]) for block in range(map_high_ref.shape[0])]
        first_ref[...] = offset_ref[...] + jnp.concatenate(moved, 1)


def across_kernel(slots, *refs):
    _, _, row = place()
    lanes = refs[-1].shape[2]
    for slot, ref in zip(slots, refs):
        refs[-1][slot] = ref[:, pl.ds(pl.multiple_of((1 - row) * lanes, LANES), lanes)]


def home_kernel(share, *refs):
    near, (*fars, filt_ref, smooth_ref, turned, tiles) = refs[: 2 * GROUP], refs[2 * GROUP :]
    outs = (filt_ref, smooth_ref)
    _, spot, row = place()
    rows = lax.axis_size("rows")
    panel, paths = outs[0].shape
    half = panel // 2
    lanes = pl.ds(pl.multiple_of(row * panel, LANES), panel)
    for kind, out_ref in enumerate(outs):
        for flip in range(GROUP):
            at = kind * GROUP + flip
            start = jnp.bitwise_xor(spot, flip) * rows
            turned[kind, pl.ds(pl.multiple_of((start + row) * share, 8), share), :] = near[at][:, lanes]
            turned[kind, pl.ds(pl.multiple_of((start + 1 - row) * share, 8), share), :] = fars[kind][flip]
        for at in range(paths // LANES):
            lines = slice(at * LANES, (at + 1) * LANES)
            for part in range(2):
                piece = turned[kind, lines, part * half : (part + 1) * half].T
                tiles[kind, at, pl.ds(part, half, stride=2), :] = piece
            out_ref[:, lines] = tiles[kind, at, 0:panel, :]


def gate(values, token, flops):
    return call(
        lambda *refs: None,
        (*values, token),
        [(value.shape, value.dtype) for value in values],
        aliases={at: at for at in range(len(values))},
        flops=flops,
    )


def body(site_rates, prior_mean, observed, obs_mask, filter_gains, smooth_gains):
    count, rows = lax.axis_size("tm"), lax.axis_size("rows")
    groups = count // GROUP
    panel, sites = filter_gains.shape[1:]
    states, paths = prior_mean.shape
    half = panel // 2
    share = paths // (GROUP * rows)
    both = ("tm", "rows")

    def swap(value, target):
        pairs = [(t * rows + r, target(t, r)) for t in range(count) for r in range(rows)]
        return lax.ppermute(value, both, pairs)

    def across(value, flip):
        return swap(value, lambda t, r: (t ^ flip) * rows + r)

    def forward(value):
        return swap(value, lambda t, r: (t ^ (2 - r)) * rows + r)

    def neighbour(value):
        return swap(value, lambda t, r: t * rows + 1 - r)

    def hop(value, source, target):
        pairs = [
            ((source * GROUP + m) * rows + r, (target * GROUP + m) * rows + r)
            for m in range(GROUP)
            for r in range(rows)
        ]
        return lax.ppermute(value, both, pairs)

    def send_home(sent):
        return [across(sent[flip], flip) for flip in reversed(range(1, GROUP))][::-1]

    *messages, own_obs, coef = call(
        functools.partial(gain_kernel, share),
        tuple(pltpu.with_memory_space_constraint(x, pltpu.HBM) for x in (site_rates.reshape(1, sites), obs_mask, filter_gains[0], observed[0])),
        [((sites + share, panel), F32)] * (GROUP - 1) + [((share, sites), F32), ((8, sites), F32)],
        [
            pltpu.VMEM((1, sites), F32),
            pltpu.VMEM((1, sites), jnp.int32),
            pltpu.VMEM((panel, sites), F32),
            pltpu.VMEM((sites, paths), F32),
            pltpu.VMEM((paths, sites), F32),
            pltpu.VMEM((sites // LANES, panel + SPARE, LANES), F32),
            pltpu.SemaphoreType.DMA((4,)),
        ],
        source=pltpu.HBM,
    )
    near = [across(value, flip) for flip, value in enumerate(messages, 1)]
    (prior,) = call(
        functools.partial(prior_kernel, share, half),
        (prior_mean,),
        [((share, states), F32)],
        [pltpu.VMEM((paths, states), F32), pltpu.VMEM((paths // LANES, states + SPARE, LANES), F32)],
    )
    pieces = call(
        smoother_gain_kernel,
        (smooth_gains[0],),
        [((states, panel), F32)],
        [pltpu.VMEM((2, states + SPARE, half), F32), pltpu.VMEM((states // LANES, panel + SPARE, LANES), F32)],
    )
    (turned_gain,) = pieces
    gain_x, gain_y = across(turned_gain, 1), across(turned_gain, 2)
    own_far, prior = lax.optimization_barrier((neighbour(messages[0]), prior))
    *near, own_far, prior, turned_gain = lax.optimization_barrier((*near, own_far, prior, turned_gain))
    far = [own_far] + [neighbour(value) for value in near]
    near = [messages[0], *near]
    high, low, obs = call(
        functools.partial(gather_kernel, range(GROUP), share, sites),
        (*near, *far, own_obs),
        [((GROUP, rows, sites, panel), BF16)] * 2 + [((GROUP, share, sites), F32)],
    )
    start, filtered = prior, ()
    *joined, offset = call(
        functools.partial(joined_filter_kernel, groups),
        (coef, high, low, obs),
        [((rows, states, panel), BF16)] * 2 + [((share, states), F32)],
        flops=JP,
    )
    for turn in range(groups):
        middle = 0 < turn < groups - 1
        if middle:
            (last,) = call(
                functools.partial(jump_kernel, turn), (start, *joined, offset), [((share, states), F32)], flops=JJ
            )
            there = hop(last, turn, turn + 1)
        filtered = call(
            functools.partial(filter_kernel, turn, middle),
            (start, coef, high, low, obs, *filtered),
            [((GROUP, share, states), F32)] + [((share, states), F32)] * (GROUP + 1 - middle),
            aliases={5 + i: i for i in range(len(filtered))},
            flops=FW[min(turn,3)],
        )
        if not middle:
            *filtered, last = filtered
        if turn == 0:
            there = hop(last, 0, 1)
        if turn < groups - 1:
            start = there
        if turn == groups - 3:
            turned_gain, gain_x, gain_y = gate((turned_gain, gain_x, gain_y), last, G1)
            (gain_d,) = call(choose_kernel, (gain_x, gain_y), [((states, panel), F32)], flops=G1)
            gain_d = forward(gain_d)
            gain_near = list(gate((turned_gain, gain_x, gain_y), start, G2))
            gain_far = [neighbour(value) for value in gain_near]
        if turn == groups - 2:
            parts = call(
                functools.partial(gather_kernel, range(GROUP - 1), 0, states),
                (*gain_near, *gain_far),
                [((GROUP, rows, states, panel), BF16)] * 2,
                flops=GA,
            )
            (gain_d,) = gate((gain_d,), parts[0], G3)
            high_back, low_back = call(
                functools.partial(gather_kernel, (GROUP - 1,), 0, states),
                (gain_d, neighbour(gain_d), *parts),
                [((GROUP, rows, states, panel), BF16)] * 2,
                aliases={2: 0, 3: 1},
            )
    filtered, sent = filtered[0], filtered[1:]

    high, low = high_back, low_back
    start, packed = last, ()
    *joined, offset = call(
        functools.partial(joined_kernel, groups),
        (coef, high, low, filtered),
        [((rows, states, panel), BF16)] * 2 + [((share, states), F32)],
        flops=JF,
    )
    for turn in range(groups):
        middle = 0 < turn < groups - 1
        if middle:
            (first,) = call(
                functools.partial(jump_kernel, groups - 1 - turn), (start, *joined, offset), [((share, states), F32)]
            )
            here = hop(first, groups - 1 - turn, groups - 2 - turn)
        packed = call(
            functools.partial(smooth_kernel, turn, groups),
            (start, coef, high, low, filtered, *packed),
            [((share, states), F32)] * (GROUP + (turn == 0)),
            aliases={5 + i: i for i in range(len(packed))},
            flops=BW[1] if middle else BW[0],
        )
        if turn == 0:
            *packed, first = packed
            here = hop(first, groups - 1, groups - 2)
        if turn == groups - 2:
            sent = gate(sent, first, G4)
            sent = [sent[0], *send_home(sent)]
        if turn < groups - 1:
            start = here
    far_shape = [((GROUP, share, panel), F32)]
    smooth_near = (packed[0], *send_home(packed))
    (filt_far,) = call(functools.partial(across_kernel, range(GROUP)), sent, far_shape)
    early = (0, GROUP - 1)
    late = range(1, GROUP - 1)
    far = call(functools.partial(across_kernel, early), [smooth_near[slot] for slot in early], far_shape)
    (far,) = call(
        functools.partial(across_kernel, late),
        (*[smooth_near[slot] for slot in late], *far),
        far_shape,
        aliases={len(late): 0},
    )
    filt, smooth = call(
        functools.partial(home_kernel, share),
        (*sent, *smooth_near, neighbour(filt_far), neighbour(far)),
        [((panel, paths), F32)] * 2,
        [pltpu.VMEM((2, paths, panel), F32), pltpu.VMEM((2, paths // LANES, panel + SPARE, LANES), F32)],
    )
    return filt[None], smooth[None]


def solution(mesh):
    placed = (
        P(),
        P(),
        P("tm", None, None),
        P("tm", None),
        P("tm", "rows", None),
        P("tm", "rows", None),
    )
    return jax.shard_map(
        body,
        mesh=mesh,
        in_specs=placed,
        out_specs=(P("tm", "rows", None), P("tm", "rows", None)),
        check_vma=False,
    )
```

```python
import functools

import jax
import jax.numpy as jnp
from jax import lax
from jax.experimental import pallas as pl
from jax.experimental.pallas import tpu as pltpu
from jax.sharding import PartitionSpec as P

GROUP = 4
LANES = 128
SPARE = 8
FW = (0, 0, 10**11, 10**11)
BW = (0, 10**10)
JF = 10**11
JP = 0
JJ = 0
GA = 10**10
G1 = G2 = G3 = 10**9
G4 = 10**9
BF16 = jnp.bfloat16
F32 = jnp.float32


def call(kernel, operands, shapes, scratch=(), aliases=None, source=pltpu.VMEM, bytes_accessed=2 << 20, flops=0, grant=24 << 20):
    return pl.pallas_call(
        kernel,
        out_shape=[jax.ShapeDtypeStruct(shape, dtype) for shape, dtype in shapes],
        in_specs=[pl.BlockSpec(memory_space=source)] * len(operands),
        out_specs=[pl.BlockSpec(memory_space=pltpu.VMEM)] * len(shapes),
        scratch_shapes=list(scratch),
        input_output_aliases=aliases or {},
        compiler_params=pltpu.CompilerParams(vmem_limit_bytes=grant),
        cost_estimate=pl.CostEstimate(flops=flops, bytes_accessed=bytes_accessed, transcendentals=0),
    )(*operands)


def place():
    step = lax.axis_index("tm")
    return lax.div(step, GROUP), lax.rem(step, GROUP), lax.axis_index("rows")


def split(value):
    high = value.astype(BF16)
    return high, (value - high.astype(F32)).astype(BF16)


def multiply(value, high_ref, low_ref):
    high, low = split(value)
    count = value.shape[0]
    both = jnp.dot(jnp.concatenate([high, low], 0), high_ref, preferred_element_type=F32)
    return both[:count] + both[count:] + jnp.dot(high, low_ref, preferred_element_type=F32)


def transition(state, coef_ref, half):
    values, slopes = [], []
    for block in range(state.shape[1] // (2 * half)):
        at = 2 * half * block
        value, slope = state[:, at : at + half], state[:, at + half : at + 2 * half]
        lanes = slice(block * half, (block + 1) * half)
        values.append(coef_ref[0:1, lanes] * value + coef_ref[1:2, lanes] * slope)
        slopes.append(coef_ref[2:3, lanes] * value + coef_ref[3:4, lanes] * slope)
    moved = jnp.concatenate([part for pair in zip(values, slopes) for part in pair], 1)
    return moved, jnp.concatenate(values, 1)


def lane_tiles(value):
    return [value[:, at : at + LANES] for at in range(0, value.shape[1], LANES)]


def fetch(source, target, sem):
    copy = pltpu.make_async_copy(source, target, sem)
    copy.start()
    return copy


def gain_kernel(
    share,
    rates_hbm,
    mask_hbm,
    gain_hbm,
    obs_hbm,
    first_ref,
    second_ref,
    third_ref,
    own_ref,
    coef_ref,
    rates_ref,
    mask_ref,
    gain_ref,
    obs_ref,
    turned,
    tiles,
    sems,
):
    sent = (first_ref, second_ref, third_ref)
    copies = [
        fetch(source, target, sems.at[at])
        for at, (source, target) in enumerate(
            ((mask_hbm, mask_ref), (gain_hbm, gain_ref), (obs_hbm, obs_ref), (rates_hbm, rates_ref))
        )
    ]
    _, spot, row = place()
    panel, sites = gain_ref.shape
    half = panel // 2
    copies[0].wait()
    copies[1].wait()
    mask = mask_ref[...].astype(F32)
    for at, tile in enumerate(lane_tiles(gain_ref[...] * mask)):
        tiles[at, 0 : tile.shape[0], :] = tile
        lines = slice(at * LANES, (at + 1) * LANES)
        for part in range(2):
            piece = tiles[at, pl.ds(part, half, stride=2), :].T
            lanes = slice(part * half, (part + 1) * half)
            for ref in sent:
                ref[lines, lanes] = piece
    copies[2].wait()
    turned[...] = obs_ref[...].T
    rows = lax.axis_size("rows")

    def slice_for(flip):
        start = (jnp.bitwise_xor(spot, flip) * rows + row) * share
        return turned[pl.ds(pl.multiple_of(start, 8), share), :]

    for flip, ref in enumerate(sent, 1):
        ref[sites : sites + share, :] = slice_for(flip)
    own_ref[...] = slice_for(0)
    copies[3].wait()
    rate = rates_ref[...]
    decay = jnp.exp(-rate)
    coef_ref[0:1, :] = decay * (1.0 + rate)
    coef_ref[1:2, :] = decay
    coef_ref[2:3, :] = -decay * rate * rate
    coef_ref[3:4, :] = decay * (1.0 - rate)
    coef_ref[4:8, :] = jnp.zeros((4, sites), F32)


def prior_kernel(share, half, prior_ref, out_ref, turned, tiles):
    _, spot, row = place()
    rows = lax.axis_size("rows")
    for at, tile in enumerate(lane_tiles(prior_ref[...])):
        tiles[at, 0 : tile.shape[0], :] = tile
        for block in range(prior_ref.shape[0] // half):
            start = (block // 2) * 2 * half + block % 2
            piece = tiles[at, pl.ds(start, half, stride=2), :].T
            turned[at * LANES : (at + 1) * LANES, block * half : (block + 1) * half] = piece
    start = (spot * rows + row) * share
    out_ref[...] = turned[pl.ds(pl.multiple_of(start, 8), share), :]


def smoother_gain_kernel(gain_ref, *refs):
    parts, (turned, tiles) = refs[:-2], refs[-2:]
    depth = parts[0].shape[0]
    panel, states = gain_ref.shape
    half = panel // 2
    for at, tile in enumerate(lane_tiles(gain_ref[...])):
        tiles[at, 0 : tile.shape[0], :] = tile
        for part in range(2):
            turned[part, at * LANES : (at + 1) * LANES, :] = tiles[at, pl.ds(part, half, stride=2), :].T
    for block in range(states // half):
        start = (block // 2) * 2 * half + block % 2
        for part in range(2):
            piece = turned[part, pl.ds(start, half, stride=2), :]
            at = block * half % depth
            parts[block * half // depth][at : at + half, part * half : (part + 1) * half] = piece


def gather_kernel(flips, share, depth, *refs):
    _, spot, row = place()
    near, far, rest = refs[: len(flips)], refs[len(flips) : 2 * len(flips)], refs[2 * len(flips) :]
    high_ref, low_ref = rest[-2 - (share > 0)], rest[-1 - (share > 0)]
    for index, flip in enumerate(flips):
        at = jnp.bitwise_xor(spot, flip)
        for ref, block in ((near[index], row), (far[index], 1 - row)):
            high, low = split(ref[0:depth, :])
            high_ref[at, block] = high
            low_ref[at, block] = low
    if share:
        rest[-1][spot] = rest[0][...]
        for flip in range(1, GROUP):
            rest[-1][jnp.bitwise_xor(spot, flip)] = near[flip][depth : depth + share, :]


def choose_kernel(first_ref, second_ref, out_ref):
    _, _, row = place()

    @pl.when(row == 0)
    def _():
        out_ref[...] = first_ref[...]

    @pl.when(row != 0)
    def _():
        out_ref[...] = second_ref[...]


def pack(spot, step, refs, state):
    for flip, ref in enumerate(refs):

        @pl.when(spot == (step ^ flip))
        def _():
            ref[...] = state


def filter_steps(state, coef_ref, high_ref, low_ref, obs_ref, keep):
    half = high_ref.shape[3] // 2
    for step in range(GROUP):
        moved, values = transition(state, coef_ref, half)
        innovation = -values if obs_ref is None else obs_ref[step] - values
        update = [
            multiply(innovation, high_ref[step, block], low_ref[step, block]) for block in range(high_ref.shape[1])
        ]
        state = moved + jnp.concatenate(update, 1)
        keep(step, state)
    return state


def filter_kernel(turn, middle, start_ref, coef_ref, high_ref, low_ref, obs_ref, *rest):
    lasts = () if middle else rest[-1:]
    outs = rest[-GROUP - 1 :] if middle else rest[-GROUP - 2 : -1]
    out_ref, sent = outs[0], outs[1:]
    group, spot, _ = place()

    @pl.when(group == turn)
    def _():
        def keep(step, state):
            out_ref[step] = state
            pack(spot, step, sent, state)

        state = filter_steps(start_ref[...], coef_ref, high_ref, low_ref, obs_ref, keep)
        for ref in lasts:
            ref[...] = state


def joined_filter_kernel(groups, coef_ref, high_ref, low_ref, obs_ref, map_high_ref, map_low_ref, offset_ref):
    group, _, _ = place()

    @pl.when(jnp.logical_and(group > 0, group < groups - 1))
    def _():
        blocks, states, lanes = map_high_ref.shape
        nothing = jnp.zeros(offset_ref.shape, F32)
        offset_ref[...] = filter_steps(nothing, coef_ref, high_ref, low_ref, obs_ref, lambda *_: None)
        rows = lax.broadcasted_iota(jnp.int32, (states, states), 0)
        columns = lax.broadcasted_iota(jnp.int32, (states, states), 1)
        unit = jnp.where(rows == columns, 1.0, 0.0)
        joined = filter_steps(unit, coef_ref, high_ref, low_ref, None, lambda *_: None)
        for block in range(blocks):
            part = joined[:, block * lanes : (block + 1) * lanes]
            map_high_ref[block], map_low_ref[block] = split(part)


def smooth_steps(state, coef_ref, high_ref, low_ref, filt_ref, keep, last_group=False):
    half = high_ref.shape[3] // 2
    for step in range(GROUP - 1, -1, -1):
        filt = filt_ref[step]
        if last_group and step == GROUP - 1:
            state = filt
        else:
            change = state - transition(filt, coef_ref, half)[0]
            update = [
                multiply(change, high_ref[step, block], low_ref[step, block]) for block in range(high_ref.shape[1])
            ]
            state = filt + jnp.concatenate(update, 1)
        keep(step, state)
    return state


def smooth_kernel(turn, groups, start_ref, coef_ref, high_ref, low_ref, filt_ref, *rest):
    sent, first = (rest[-GROUP - 1 : -1], rest[-1:]) if turn == 0 else (rest[-GROUP:], ())
    group, spot, _ = place()

    @pl.when(group == groups - 1 - turn)
    def _():
        keep = lambda step, state: pack(spot, step, sent, state)
        state = smooth_steps(start_ref[...], coef_ref, high_ref, low_ref, filt_ref, keep, turn == 0)
        for ref in first:
            ref[...] = state


def joined_kernel(groups, coef_ref, high_ref, low_ref, filt_ref, map_high_ref, map_low_ref, offset_ref):
    group, _, _ = place()

    @pl.when(jnp.logical_and(group > 0, group < groups - 1))
    def _():
        blocks, lanes = high_ref.shape[1], high_ref.shape[3]
        nothing = jnp.zeros(offset_ref.shape, F32)
        offset_ref[...] = smooth_steps(nothing, coef_ref, high_ref, low_ref, filt_ref, lambda *_: None)
        last = GROUP - 1
        joined = [high_ref[last, block].astype(F32) + low_ref[last, block].astype(F32) for block in range(blocks)]
        for step in range(GROUP - 2, -1, -1):
            whole = jnp.concatenate(joined, 1)
            joined = [multiply(whole, high_ref[step, block], low_ref[step, block]) for block in range(blocks)]
        for block in range(blocks):
            map_high_ref[block], map_low_ref[block] = split(joined[block])


def jump_kernel(active, start_ref, map_high_ref, map_low_ref, offset_ref, first_ref):
    group, _, _ = place()

    @pl.when(group == active)
    def _():
        start = start_ref[...]
        moved = [multiply(start, map_high_ref[block], map_low_ref[block]) for block in range(map_high_ref.shape[0])]
        first_ref[...] = offset_ref[...] + jnp.concatenate(moved, 1)


def across_kernel(slots, *refs):
    _, _, row = place()
    lanes = refs[-1].shape[2]
    for slot, ref in zip(slots, refs):
        refs[-1][slot] = ref[:, pl.ds(pl.multiple_of((1 - row) * lanes, LANES), lanes)]


def home_kernel(share, *refs):
    near, (*fars, filt_ref, smooth_ref, turned, tiles) = refs[: 2 * GROUP], refs[2 * GROUP :]
    outs = (filt_ref, smooth_ref)
    _, spot, row = place()
    rows = lax.axis_size("rows")
    panel, paths = outs[0].shape
    half = panel // 2
    lanes = pl.ds(pl.multiple_of(row * panel, LANES), panel)
    for kind, out_ref in enumerate(outs):
        for flip in range(GROUP):
            at = kind * GROUP + flip
            start = jnp.bitwise_xor(spot, flip) * rows
            turned[kind, pl.ds(pl.multiple_of((start + row) * share, 8), share), :] = near[at][:, lanes]
            turned[kind, pl.ds(pl.multiple_of((start + 1 - row) * share, 8), share), :] = fars[kind][flip]
        for at in range(paths // LANES):
            lines = slice(at * LANES, (at + 1) * LANES)
            for part in range(2):
                piece = turned[kind, lines, part * half : (part + 1) * half].T
                tiles[kind, at, pl.ds(part, half, stride=2), :] = piece
            out_ref[:, lines] = tiles[kind, at, 0:panel, :]


def gate(values, token, flops):
    return call(
        lambda *refs: None,
        (*values, token),
        [(value.shape, value.dtype) for value in values],
        aliases={at: at for at in range(len(values))},
        flops=flops,
    )


def body(site_rates, prior_mean, observed, obs_mask, filter_gains, smooth_gains):
    count, rows = lax.axis_size("tm"), lax.axis_size("rows")
    groups = count // GROUP
    panel, sites = filter_gains.shape[1:]
    states, paths = prior_mean.shape
    half = panel // 2
    share = paths // (GROUP * rows)
    both = ("tm", "rows")

    def swap(value, target):
        pairs = [(t * rows + r, target(t, r)) for t in range(count) for r in range(rows)]
        return lax.ppermute(value, both, pairs)

    def across(value, flip):
        return swap(value, lambda t, r: (t ^ flip) * rows + r)

    def forward(value):
        return swap(value, lambda t, r: (t ^ (2 - r)) * rows + r)

    def neighbour(value):
        return swap(value, lambda t, r: t * rows + 1 - r)

    def hop(value, source, target):
        pairs = [(g, g ^ 1) for g in range(groups)] if source ^ 1 == target and groups % 2 == 0 else [(source, target)]
        return lax.ppermute(
            value,
            both,
            [
                ((here * GROUP + m) * rows + r, (there * GROUP + m) * rows + r)
                for here, there in pairs
                for m in range(GROUP)
                for r in range(rows)
            ],
        )

    def send_home(sent):
        return [across(sent[flip], flip) for flip in reversed(range(1, GROUP))][::-1]

    *messages, own_obs, coef = call(
        functools.partial(gain_kernel, share),
        tuple(pltpu.with_memory_space_constraint(x, pltpu.HBM) for x in (site_rates.reshape(1, sites), obs_mask, filter_gains[0], observed[0])),
        [((sites + share, panel), F32)] * (GROUP - 1) + [((share, sites), F32), ((8, sites), F32)],
        [
            pltpu.VMEM((1, sites), F32),
            pltpu.VMEM((1, sites), jnp.int32),
            pltpu.VMEM((panel, sites), F32),
            pltpu.VMEM((sites, paths), F32),
            pltpu.VMEM((paths, sites), F32),
            pltpu.VMEM((sites // LANES, panel + SPARE, LANES), F32),
            pltpu.SemaphoreType.DMA((4,)),
        ],
        source=pltpu.HBM,
    )
    near = [across(value, flip) for flip, value in enumerate(messages, 1)]
    (prior,) = call(
        functools.partial(prior_kernel, share, half),
        (prior_mean,),
        [((share, states), F32)],
        [pltpu.VMEM((paths, states), F32), pltpu.VMEM((paths // LANES, states + SPARE, LANES), F32)],
    )
    pieces = call(
        smoother_gain_kernel,
        (smooth_gains[0],),
        [((states, panel), F32)],
        [pltpu.VMEM((2, states + SPARE, half), F32), pltpu.VMEM((states // LANES, panel + SPARE, LANES), F32)],
    )
    (turned_gain,) = pieces
    gain_x, gain_y = across(turned_gain, 1), across(turned_gain, 2)
    own_far, prior = lax.optimization_barrier((neighbour(messages[0]), prior))
    *near, own_far, prior, turned_gain = lax.optimization_barrier((*near, own_far, prior, turned_gain))
    far = [own_far] + [neighbour(value) for value in near]
    near = [messages[0], *near]
    high, low, obs = call(
        functools.partial(gather_kernel, range(GROUP), share, sites),
        (*near, *far, own_obs),
        [((GROUP, rows, sites, panel), BF16)] * 2 + [((GROUP, share, sites), F32)],
    )
    start, filtered = prior, ()
    *joined, offset = call(
        functools.partial(joined_filter_kernel, groups),
        (coef, high, low, obs),
        [((rows, states, panel), BF16)] * 2 + [((share, states), F32)],
        flops=JP,
    )
    for turn in range(groups):
        middle = 0 < turn < groups - 1
        if middle:
            (last,) = call(
                functools.partial(jump_kernel, turn), (start, *joined, offset), [((share, states), F32)], flops=JJ
            )
            there = hop(last, turn, turn + 1)
        filtered = call(
            functools.partial(filter_kernel, turn, middle),
            (start, coef, high, low, obs, *filtered),
            [((GROUP, share, states), F32)] + [((share, states), F32)] * (GROUP + 1 - middle),
            aliases={5 + i: i for i in range(len(filtered))},
            flops=FW[min(turn,3)],
        )
        if not middle:
            *filtered, last = filtered
        if turn == 0:
            there = hop(last, 0, 1)
        if turn < groups - 1:
            start = there
        if turn == groups - 3:
            turned_gain, gain_x, gain_y = gate((turned_gain, gain_x, gain_y), last, G1)
            (gain_d,) = call(choose_kernel, (gain_x, gain_y), [((states, panel), F32)], flops=G1)
            gain_d = forward(gain_d)
            gain_near = list(gate((turned_gain, gain_x, gain_y), start, G2))
            gain_far = [neighbour(value) for value in gain_near]
        if turn == groups - 2:
            parts = call(
                functools.partial(gather_kernel, range(GROUP - 1), 0, states),
                (*gain_near, *gain_far),
                [((GROUP, rows, states, panel), BF16)] * 2,
                flops=GA,
            )
            (gain_d,) = gate((gain_d,), parts[0], G3)
            high_back, low_back = call(
                functools.partial(gather_kernel, (GROUP - 1,), 0, states),
                (gain_d, neighbour(gain_d), *parts),
                [((GROUP, rows, states, panel), BF16)] * 2,
                aliases={2: 0, 3: 1},
            )
    filtered, sent = filtered[0], filtered[1:]

    high, low = high_back, low_back
    start, packed = last, ()
    *joined, offset = call(
        functools.partial(joined_kernel, groups),
        (coef, high, low, filtered),
        [((rows, states, panel), BF16)] * 2 + [((share, states), F32)],
        flops=JF,
    )
    for turn in range(groups):
        middle = 0 < turn < groups - 1
        if middle:
            (first,) = call(
                functools.partial(jump_kernel, groups - 1 - turn), (start, *joined, offset), [((share, states), F32)]
            )
            here = hop(first, groups - 1 - turn, groups - 2 - turn)
        packed = call(
            functools.partial(smooth_kernel, turn, groups),
            (start, coef, high, low, filtered, *packed),
            [((share, states), F32)] * (GROUP + (turn == 0)),
            aliases={5 + i: i for i in range(len(packed))},
            flops=BW[1] if middle else BW[0],
        )
        if turn == 0:
            *packed, first = packed
            here = hop(first, groups - 1, groups - 2)
        if turn == groups - 2:
            sent = gate(sent, first, G4)
            sent = [sent[0], *send_home(sent)]
        if turn < groups - 1:
            start = here
    far_shape = [((GROUP, share, panel), F32)]
    smooth_near = (packed[0], *send_home(packed))
    (filt_far,) = call(functools.partial(across_kernel, range(GROUP)), sent, far_shape)
    early = (0, GROUP - 1)
    late = range(1, GROUP - 1)
    far = call(functools.partial(across_kernel, early), [smooth_near[slot] for slot in early], far_shape)
    (far,) = call(
        functools.partial(across_kernel, late),
        (*[smooth_near[slot] for slot in late], *far),
        far_shape,
        aliases={len(late): 0},
    )
    filt, smooth = call(
        functools.partial(home_kernel, share),
        (*sent, *smooth_near, neighbour(filt_far), neighbour(far)),
        [((panel, paths), F32)] * 2,
        [pltpu.VMEM((2, paths, panel), F32), pltpu.VMEM((2, paths // LANES, panel + SPARE, LANES), F32)],
    )
    return filt[None], smooth[None]


def solution(mesh):
    placed = (
        P(),
        P(),
        P("tm", None, None),
        P("tm", None),
        P("tm", "rows", None),
        P("tm", "rows", None),
    )
    return jax.shard_map(
        body,
        mesh=mesh,
        in_specs=placed,
        out_specs=(P("tm", "rows", None), P("tm", "rows", None)),
        check_vma=False,
    )
```

```python
import functools

import jax
import jax.numpy as jnp
from jax import lax
from jax.experimental import pallas as pl
from jax.experimental.pallas import tpu as pltpu
from jax.sharding import PartitionSpec as P

GROUP = 4
LANES = 128
SPARE = 8
FW = (0, 0, 10**11, 10**11)
BW = (0, 10**10)
JF = 10**11
JP = 0
JJ = 0
GA = 10**10
G1 = G2 = G3 = 10**9
G4 = 10**9
BF16 = jnp.bfloat16
F32 = jnp.float32


def call(kernel, operands, shapes, scratch=(), aliases=None, source=pltpu.VMEM, bytes_accessed=2 << 20, flops=0, grant=24 << 20):
    return pl.pallas_call(
        kernel,
        out_shape=[jax.ShapeDtypeStruct(shape, dtype) for shape, dtype in shapes],
        in_specs=[pl.BlockSpec(memory_space=source)] * len(operands),
        out_specs=[pl.BlockSpec(memory_space=pltpu.VMEM)] * len(shapes),
        scratch_shapes=list(scratch),
        input_output_aliases=aliases or {},
        compiler_params=pltpu.CompilerParams(vmem_limit_bytes=grant),
        cost_estimate=pl.CostEstimate(flops=flops, bytes_accessed=bytes_accessed, transcendentals=0),
    )(*operands)


def place():
    step = lax.axis_index("tm")
    return lax.div(step, GROUP), lax.rem(step, GROUP), lax.axis_index("rows")


def split(value):
    high = value.astype(BF16)
    return high, (value - high.astype(F32)).astype(BF16)


def multiply(value, high_ref, low_ref):
    high, low = split(value)
    count = value.shape[0]
    both = jnp.dot(jnp.concatenate([high, low], 0), high_ref, preferred_element_type=F32)
    return both[:count] + both[count:] + jnp.dot(high, low_ref, preferred_element_type=F32)


def transition(state, coef_ref, half):
    values, slopes = [], []
    for block in range(state.shape[1] // (2 * half)):
        at = 2 * half * block
        value, slope = state[:, at : at + half], state[:, at + half : at + 2 * half]
        lanes = slice(block * half, (block + 1) * half)
        values.append(coef_ref[0:1, lanes] * value + coef_ref[1:2, lanes] * slope)
        slopes.append(coef_ref[2:3, lanes] * value + coef_ref[3:4, lanes] * slope)
    moved = jnp.concatenate([part for pair in zip(values, slopes) for part in pair], 1)
    return moved, jnp.concatenate(values, 1)


def lane_tiles(value):
    return [value[:, at : at + LANES] for at in range(0, value.shape[1], LANES)]


def fetch(source, target, sem):
    copy = pltpu.make_async_copy(source, target, sem)
    copy.start()
    return copy


def gain_kernel(
    share,
    rates_hbm,
    mask_hbm,
    gain_hbm,
    obs_hbm,
    first_ref,
    second_ref,
    third_ref,
    own_ref,
    coef_ref,
    rates_ref,
    mask_ref,
    gain_ref,
    obs_ref,
    turned,
    tiles,
    sems,
):
    sent = (first_ref, second_ref, third_ref)
    copies = [
        fetch(source, target, sems.at[at])
        for at, (source, target) in enumerate(
            ((mask_hbm, mask_ref), (gain_hbm, gain_ref), (obs_hbm, obs_ref), (rates_hbm, rates_ref))
        )
    ]
    _, spot, row = place()
    panel, sites = gain_ref.shape
    half = panel // 2
    copies[0].wait()
    copies[1].wait()
    mask = mask_ref[...].astype(F32)
    for at, tile in enumerate(lane_tiles(gain_ref[...] * mask)):
        tiles[at, 0 : tile.shape[0], :] = tile
        lines = slice(at * LANES, (at + 1) * LANES)
        for part in range(2):
            piece = tiles[at, pl.ds(part, half, stride=2), :].T
            lanes = slice(part * half, (part + 1) * half)
            for ref in sent:
                ref[lines, lanes] = piece
    copies[2].wait()
    turned[...] = obs_ref[...].T
    rows = lax.axis_size("rows")

    def slice_for(flip):
        start = (jnp.bitwise_xor(spot, flip) * rows + row) * share
        return turned[pl.ds(pl.multiple_of(start, 8), share), :]

    for flip, ref in enumerate(sent, 1):
        ref[sites : sites + share, :] = slice_for(flip)
    own_ref[...] = slice_for(0)
    copies[3].wait()
    rate = rates_ref[...]
    decay = jnp.exp(-rate)
    coef_ref[0:1, :] = decay * (1.0 + rate)
    coef_ref[1:2, :] = decay
    coef_ref[2:3, :] = -decay * rate * rate
    coef_ref[3:4, :] = decay * (1.0 - rate)
    coef_ref[4:8, :] = jnp.zeros((4, sites), F32)


def prior_kernel(share, half, prior_ref, out_ref, turned, tiles):
    _, spot, row = place()
    rows = lax.axis_size("rows")
    for at, tile in enumerate(lane_tiles(prior_ref[...])):
        tiles[at, 0 : tile.shape[0], :] = tile
        for block in range(prior_ref.shape[0] // half):
            start = (block // 2) * 2 * half + block % 2
            piece = tiles[at, pl.ds(start, half, stride=2), :].T
            turned[at * LANES : (at + 1) * LANES, block * half : (block + 1) * half] = piece
    start = (spot * rows + row) * share
    out_ref[...] = turned[pl.ds(pl.multiple_of(start, 8), share), :]


def smoother_gain_kernel(gain_ref, *refs):
    parts, (turned, tiles) = refs[:-2], refs[-2:]
    depth = parts[0].shape[0]
    panel, states = gain_ref.shape
    half = panel // 2
    for at, tile in enumerate(lane_tiles(gain_ref[...])):
        tiles[at, 0 : tile.shape[0], :] = tile
        for part in range(2):
            turned[part, at * LANES : (at + 1) * LANES, :] = tiles[at, pl.ds(part, half, stride=2), :].T
    for block in range(states // half):
        start = (block // 2) * 2 * half + block % 2
        for part in range(2):
            piece = turned[part, pl.ds(start, half, stride=2), :]
            at = block * half % depth
            parts[block * half // depth][at : at + half, part * half : (part + 1) * half] = piece


def gather_kernel(flips, share, depth, *refs):
    _, spot, row = place()
    near, far, rest = refs[: len(flips)], refs[len(flips) : 2 * len(flips)], refs[2 * len(flips) :]
    high_ref, low_ref = rest[-2 - (share > 0)], rest[-1 - (share > 0)]
    for index, flip in enumerate(flips):
        at = jnp.bitwise_xor(spot, flip)
        for ref, block in ((near[index], row), (far[index], 1 - row)):
            high, low = split(ref[0:depth, :])
            high_ref[at, block] = high
            low_ref[at, block] = low
    if share:
        rest[-1][spot] = rest[0][...]
        for flip in range(1, GROUP):
            rest[-1][jnp.bitwise_xor(spot, flip)] = near[flip][depth : depth + share, :]


def choose_kernel(first_ref, second_ref, out_ref):
    _, _, row = place()

    @pl.when(row == 0)
    def _():
        out_ref[...] = first_ref[...]

    @pl.when(row != 0)
    def _():
        out_ref[...] = second_ref[...]


def pack(spot, step, refs, state):
    for flip, ref in enumerate(refs):

        @pl.when(spot == (step ^ flip))
        def _():
            ref[...] = state


def filter_steps(state, coef_ref, high_ref, low_ref, obs_ref, keep):
    half = high_ref.shape[3] // 2
    for step in range(GROUP):
        moved, values = transition(state, coef_ref, half)
        innovation = -values if obs_ref is None else obs_ref[step] - values
        update = [
            multiply(innovation, high_ref[step, block], low_ref[step, block]) for block in range(high_ref.shape[1])
        ]
        state = moved + jnp.concatenate(update, 1)
        keep(step, state)
    return state


def filter_kernel(turn, middle, start_ref, coef_ref, high_ref, low_ref, obs_ref, *rest):
    lasts = () if middle else rest[-1:]
    outs = rest[-GROUP - 1 :] if middle else rest[-GROUP - 2 : -1]
    out_ref, sent = outs[0], outs[1:]
    group, spot, _ = place()

    @pl.when(group == turn)
    def _():
        def keep(step, state):
            out_ref[step] = state
            pack(spot, step, sent, state)

        state = filter_steps(start_ref[...], coef_ref, high_ref, low_ref, obs_ref, keep)
        for ref in lasts:
            ref[...] = state


def joined_filter_kernel(groups, coef_ref, high_ref, low_ref, obs_ref, map_high_ref, map_low_ref, offset_ref):
    group, _, _ = place()

    @pl.when(jnp.logical_and(group > 0, group < groups - 1))
    def _():
        blocks, states, lanes = map_high_ref.shape
        nothing = jnp.zeros(offset_ref.shape, F32)
        offset_ref[...] = filter_steps(nothing, coef_ref, high_ref, low_ref, obs_ref, lambda *_: None)
        rows = lax.broadcasted_iota(jnp.int32, (states, states), 0)
        columns = lax.broadcasted_iota(jnp.int32, (states, states), 1)
        unit = jnp.where(rows == columns, 1.0, 0.0)
        joined = filter_steps(unit, coef_ref, high_ref, low_ref, None, lambda *_: None)
        for block in range(blocks):
            part = joined[:, block * lanes : (block + 1) * lanes]
            map_high_ref[block], map_low_ref[block] = split(part)


def smooth_steps(state, coef_ref, high_ref, low_ref, filt_ref, keep, last_group=False):
    half = high_ref.shape[3] // 2
    for step in range(GROUP - 1, -1, -1):
        filt = filt_ref[step]
        if last_group and step == GROUP - 1:
            state = filt
        else:
            change = state - transition(filt, coef_ref, half)[0]
            update = [
                multiply(change, high_ref[step, block], low_ref[step, block]) for block in range(high_ref.shape[1])
            ]
            state = filt + jnp.concatenate(update, 1)
        keep(step, state)
    return state


def smooth_kernel(turn, groups, start_ref, coef_ref, high_ref, low_ref, filt_ref, *rest):
    sent, first = (rest[-GROUP - 1 : -1], rest[-1:]) if turn == 0 else (rest[-GROUP:], ())
    group, spot, _ = place()

    @pl.when(group == groups - 1 - turn)
    def _():
        keep = lambda step, state: pack(spot, step, sent, state)
        state = smooth_steps(start_ref[...], coef_ref, high_ref, low_ref, filt_ref, keep, turn == 0)
        for ref in first:
            ref[...] = state


def joined_kernel(groups, coef_ref, high_ref, low_ref, filt_ref, map_high_ref, map_low_ref, offset_ref):
    group, _, _ = place()

    @pl.when(jnp.logical_and(group > 0, group < groups - 1))
    def _():
        blocks, lanes = high_ref.shape[1], high_ref.shape[3]
        nothing = jnp.zeros(offset_ref.shape, F32)
        offset_ref[...] = smooth_steps(nothing, coef_ref, high_ref, low_ref, filt_ref, lambda *_: None)
        last = GROUP - 1
        joined = [high_ref[last, block].astype(F32) + low_ref[last, block].astype(F32) for block in range(blocks)]
        for step in range(GROUP - 2, -1, -1):
            whole = jnp.concatenate(joined, 1)
            joined = [multiply(whole, high_ref[step, block], low_ref[step, block]) for block in range(blocks)]
        for block in range(blocks):
            map_high_ref[block], map_low_ref[block] = split(joined[block])


def jump_kernel(active, start_ref, map_high_ref, map_low_ref, offset_ref, first_ref):
    group, _, _ = place()

    @pl.when(group == active)
    def _():
        start = start_ref[...]
        moved = [multiply(start, map_high_ref[block], map_low_ref[block]) for block in range(map_high_ref.shape[0])]
        first_ref[...] = offset_ref[...] + jnp.concatenate(moved, 1)


def across_kernel(slots, *refs):
    _, _, row = place()
    lanes = refs[-1].shape[2]
    for slot, ref in zip(slots, refs):
        refs[-1][slot] = ref[:, pl.ds(pl.multiple_of((1 - row) * lanes, LANES), lanes)]


def home_kernel(share, *refs):
    near, (*fars, filt_ref, smooth_ref, turned, tiles) = refs[: 2 * GROUP], refs[2 * GROUP :]
    outs = (filt_ref, smooth_ref)
    _, spot, row = place()
    rows = lax.axis_size("rows")
    panel, paths = outs[0].shape
    half = panel // 2
    lanes = pl.ds(pl.multiple_of(row * panel, LANES), panel)
    for kind, out_ref in enumerate(outs):
        for flip in range(GROUP):
            at = kind * GROUP + flip
            start = jnp.bitwise_xor(spot, flip) * rows
            turned[kind, pl.ds(pl.multiple_of((start + row) * share, 8), share), :] = near[at][:, lanes]
            turned[kind, pl.ds(pl.multiple_of((start + 1 - row) * share, 8), share), :] = fars[kind][flip]
        for at in range(paths // LANES):
            lines = slice(at * LANES, (at + 1) * LANES)
            for part in range(2):
                piece = turned[kind, lines, part * half : (part + 1) * half].T
                tiles[kind, at, pl.ds(part, half, stride=2), :] = piece
            out_ref[:, lines] = tiles[kind, at, 0:panel, :]


def gate(values, token, flops):
    return call(
        lambda *refs: None,
        (*values, token),
        [(value.shape, value.dtype) for value in values],
        aliases={at: at for at in range(len(values))},
        flops=flops,
    )


def body(site_rates, prior_mean, observed, obs_mask, filter_gains, smooth_gains):
    count, rows = lax.axis_size("tm"), lax.axis_size("rows")
    groups = count // GROUP
    panel, sites = filter_gains.shape[1:]
    states, paths = prior_mean.shape
    half = panel // 2
    share = paths // (GROUP * rows)
    both = ("tm", "rows")

    def swap(value, target):
        pairs = [(t * rows + r, target(t, r)) for t in range(count) for r in range(rows)]
        return lax.ppermute(value, both, pairs)

    def across(value, flip):
        return swap(value, lambda t, r: (t ^ flip) * rows + r)

    def forward(value):
        return swap(value, lambda t, r: (t ^ (2 - r)) * rows + r)

    def neighbour(value):
        return swap(value, lambda t, r: t * rows + 1 - r)

    def hop(value, source, target):
        pairs = [(g, g ^ 1) for g in range(groups)] if source ^ 1 == target and groups % 2 == 0 else [(source, target)]
        return lax.ppermute(
            value,
            both,
            [
                ((here * GROUP + m) * rows + r, (there * GROUP + m) * rows + r)
                for here, there in pairs
                for m in range(GROUP)
                for r in range(rows)
            ],
        )

    def send_home(sent):
        return [across(sent[flip], flip) for flip in reversed(range(1, GROUP))][::-1]

    *messages, own_obs, coef = call(
        functools.partial(gain_kernel, share),
        tuple(pltpu.with_memory_space_constraint(x, pltpu.HBM) for x in (site_rates.reshape(1, sites), obs_mask, filter_gains[0], observed[0])),
        [((sites + share, panel), F32)] * (GROUP - 1) + [((share, sites), F32), ((8, sites), F32)],
        [
            pltpu.VMEM((1, sites), F32),
            pltpu.VMEM((1, sites), jnp.int32),
            pltpu.VMEM((panel, sites), F32),
            pltpu.VMEM((sites, paths), F32),
            pltpu.VMEM((paths, sites), F32),
            pltpu.VMEM((sites // LANES, panel + SPARE, LANES), F32),
            pltpu.SemaphoreType.DMA((4,)),
        ],
        source=pltpu.HBM,
    )
    near = [across(value, flip) for flip, value in enumerate(messages, 1)]
    (prior,) = call(
        functools.partial(prior_kernel, share, half),
        (prior_mean,),
        [((share, states), F32)],
        [pltpu.VMEM((paths, states), F32), pltpu.VMEM((paths // LANES, states + SPARE, LANES), F32)],
    )
    pieces = call(
        smoother_gain_kernel,
        (smooth_gains[0],),
        [((states, panel), F32)],
        [pltpu.VMEM((2, states + SPARE, half), F32), pltpu.VMEM((states // LANES, panel + SPARE, LANES), F32)],
    )
    (turned_gain,) = pieces
    gain_x, gain_y = across(turned_gain, 1), across(turned_gain, 2)
    *near, prior, turned_gain = lax.optimization_barrier((*near, prior, turned_gain))
    near = [messages[0], *near]
    far = [neighbour(value) for value in near]
    high, low, obs = call(
        functools.partial(gather_kernel, range(GROUP), share, sites),
        (*near, *far, own_obs),
        [((GROUP, rows, sites, panel), BF16)] * 2 + [((GROUP, share, sites), F32)],
    )
    start, filtered = prior, ()
    *joined, offset = call(
        functools.partial(joined_filter_kernel, groups),
        (coef, high, low, obs),
        [((rows, states, panel), BF16)] * 2 + [((share, states), F32)],
        flops=JP,
    )
    for turn in range(groups):
        middle = 0 < turn < groups - 1
        if middle:
            (last,) = call(
                functools.partial(jump_kernel, turn), (start, *joined, offset), [((share, states), F32)], flops=JJ
            )
            there = hop(last, turn, turn + 1)
        filtered = call(
            functools.partial(filter_kernel, turn, middle),
            (start, coef, high, low, obs, *filtered),
            [((GROUP, share, states), F32)] + [((share, states), F32)] * (GROUP + 1 - middle),
            aliases={5 + i: i for i in range(len(filtered))},
            flops=FW[min(turn,3)],
        )
        if not middle:
            *filtered, last = filtered
        if turn == 0:
            there = hop(last, 0, 1)
        if turn < groups - 1:
            start = there
        if turn == groups - 3:
            turned_gain, gain_x, gain_y = gate((turned_gain, gain_x, gain_y), last, G1)
            (gain_d,) = call(choose_kernel, (gain_x, gain_y), [((states, panel), F32)], flops=G1)
            gain_d = forward(gain_d)
            gain_near = list(gate((turned_gain, gain_x, gain_y), start, G2))
            gain_far = [neighbour(value) for value in gain_near]
        if turn == groups - 2:
            parts = call(
                functools.partial(gather_kernel, range(GROUP - 1), 0, states),
                (*gain_near, *gain_far),
                [((GROUP, rows, states, panel), BF16)] * 2,
                flops=GA,
            )
            (gain_d,) = gate((gain_d,), parts[0], G3)
            high_back, low_back = call(
                functools.partial(gather_kernel, (GROUP - 1,), 0, states),
                (gain_d, neighbour(gain_d), *parts),
                [((GROUP, rows, states, panel), BF16)] * 2,
                aliases={2: 0, 3: 1},
            )
    filtered, sent = filtered[0], filtered[1:]

    high, low = high_back, low_back
    start, packed = last, ()
    *joined, offset = call(
        functools.partial(joined_kernel, groups),
        (coef, high, low, filtered),
        [((rows, states, panel), BF16)] * 2 + [((share, states), F32)],
        flops=JF,
    )
    for turn in range(groups):
        middle = 0 < turn < groups - 1
        if middle:
            (first,) = call(
                functools.partial(jump_kernel, groups - 1 - turn), (start, *joined, offset), [((share, states), F32)]
            )
            here = hop(first, groups - 1 - turn, groups - 2 - turn)
        packed = call(
            functools.partial(smooth_kernel, turn, groups),
            (start, coef, high, low, filtered, *packed),
            [((share, states), F32)] * (GROUP + (turn == 0)),
            aliases={5 + i: i for i in range(len(packed))},
            flops=BW[1] if middle else BW[0],
        )
        if turn == 0:
            *packed, first = packed
            here = hop(first, groups - 1, groups - 2)
        if turn == groups - 2:
            sent = gate(sent, first, G4)
            sent = [sent[0], *send_home(sent)]
        if turn < groups - 1:
            start = here
    far_shape = [((GROUP, share, panel), F32)]
    smooth_near = (packed[0], *send_home(packed))
    (filt_far,) = call(functools.partial(across_kernel, range(GROUP)), sent, far_shape)
    early = (0, GROUP - 1)
    late = range(1, GROUP - 1)
    far = call(functools.partial(across_kernel, early), [smooth_near[slot] for slot in early], far_shape)
    (far,) = call(
        functools.partial(across_kernel, late),
        (*[smooth_near[slot] for slot in late], *far),
        far_shape,
        aliases={len(late): 0},
    )
    filt, smooth = call(
        functools.partial(home_kernel, share),
        (*sent, *smooth_near, neighbour(filt_far), neighbour(far)),
        [((panel, paths), F32)] * 2,
        [pltpu.VMEM((2, paths, panel), F32), pltpu.VMEM((2, paths // LANES, panel + SPARE, LANES), F32)],
    )
    return filt[None], smooth[None]


def solution(mesh):
    placed = (
        P(),
        P(),
        P("tm", None, None),
        P("tm", None),
        P("tm", "rows", None),
        P("tm", "rows", None),
    )
    return jax.shard_map(
        body,
        mesh=mesh,
        in_specs=placed,
        out_specs=(P("tm", "rows", None), P("tm", "rows", None)),
        check_vma=False,
    )
```
